256 devices in a mesh: source: 32 (over z, y), row: 4 (over x), cond: 2 (over core).
Axes of the slice: x: 4, y: 4, z: 8, core: 2. Of those that a mesh axis runs over, the one named last changes fastest.
Arguments:
- spectrum: bfloat16 [2, 1024, 1024], P(None, ('source', 'row')), may hold values from -0.046875 to 0.046875
- centers: float32 [32, 2], P('source'), may hold values from 0 to 1024
- blocks: int32 [32, 8], P('source'), may hold values from 0 to 63, as said below
- counts: int32 [32], P('source'), may hold values from 1 to 8
- weights: float32 [32], P('source'), may hold values from 0.2 to 1
- defocus: float32 [4], P('cond'), may hold values from -3 to 3
- dose_scale: float32 [4], P('cond'), may hold values from 0.5 to 2
Outputs:
- soft_slope: float32 [512, 4096], P('row', 'source')
The draws below stay inside these ranges and needn't reach their ends.
Inputs may be any that keep to these rules, and one draw needn't show every extreme that they name: `blocks`: the entries of one row are distinct block numbers; entries of row s past counts[s] are not used.
All inputs are finite; a program needn't handle non-finite values.
Results may differ from the reference program's by a relative error of at most 0.00035.
The reference program's roundings to bfloat16 on the way count: a program that leaves them out, or rounds other values in their place, can miss the bound.
Values may be sent and summed in bfloat16 or wider, within the bound.
No kernel may reach another device: no remote copies, remote signals or barrier semaphores. Data moves between devices by JAX's collectives and lax.ppermute only.
A program may use at most 64 MiB of HBM per device.

```python
import math
import jax
import jax.numpy as jnp
from jax import lax

N = 4096
BLOCK = 128
NB = 8
B_MAX = 8
SPEC = 1024
SOURCES = 32
CONDS = 4
X = 512


def anchor_blocks(key):
    drawn = jax.random.randint(key, (SOURCES, 2), 0, NB, dtype=jnp.int32)
    pick_key = jax.random.fold_in(key, 97)
    first_key, second_key = jax.random.split(pick_key)
    lowest = jax.random.randint(first_key, (), 0, SOURCES, dtype=jnp.int32)
    step = jax.random.randint(second_key, (), 1, SOURCES, dtype=jnp.int32)
    highest = (lowest + step) % SOURCES
    drawn = drawn.at[lowest].set(jnp.zeros((2,), jnp.int32))
    drawn = drawn.at[highest].set(jnp.full((2,), NB - 1, jnp.int32))
    return drawn


def draw_centers(key, part):
    anchor = anchor_blocks(key)
    key = jax.random.fold_in(key, 5)
    offset = jax.random.uniform(key, (SOURCES, 2), jnp.float32, 0.0, 1.0)
    return (anchor.astype(jnp.float32) + offset) * BLOCK


def draw_blocks(key, part):
    anchor = anchor_blocks(key)
    key = jax.random.fold_in(key, 11)
    numbers = jnp.arange(NB * NB, dtype=jnp.int32)
    row_gap = (numbers // NB)[None, :] - anchor[:, 0:1]
    col_gap = (numbers % NB)[None, :] - anchor[:, 1:2]
    distance = row_gap * row_gap + col_gap * col_gap
    source_keys = jax.random.split(key, SOURCES)
    tiebreak = jax.vmap(lambda single: jax.random.permutation(single, NB * NB))(source_keys).astype(jnp.int32)
    score = distance * (NB * NB) + tiebreak
    order = jnp.argsort(score, axis=1, stable=True)
    return order[:, :B_MAX].astype(jnp.int32)


def draw_counts(key, part):
    key = jax.random.fold_in(key, 23)
    first_key, second_key = jax.random.split(key)
    drawn = jax.random.randint(first_key, (SOURCES,), 1, B_MAX + 1, dtype=jnp.int32)
    fullest = jax.random.randint(second_key, (), 0, SOURCES, dtype=jnp.int32)
    return drawn.at[fullest].set(B_MAX)


def shard_levels(rng, shape, shards, low, top_value):
    factor_of, own = 1.0, jax.random.fold_in(rng, 6)
    for position, parts in shards:
        draws = jnp.exp(jax.random.uniform(jax.random.fold_in(own, position), (parts,), jnp.float32, low / len(shards), top_value / len(shards)))
        factor_of = factor_of * jnp.repeat(draws, shape[position] // parts).reshape([-1 if axis == position else 1 for axis in range(len(shape))])
    return factor_of


def noise(rng, extent, scale, bound, cuts=(), kind=jnp.bfloat16):
    factor_of = shard_levels(rng, extent, cuts, -0.22, 0.18) if cuts else 1.0
    array = jax.random.normal(rng, extent, jnp.float32) * scale * factor_of
    return jnp.minimum(jnp.maximum(array, -bound), bound).astype(kind)


def setup_inputs(seed: int = 0) -> dict:
    arg_keys = jax.random.split(jax.random.key(seed), 8)
    spectrum = noise(arg_keys[0], (2, SPEC, SPEC), (1.0 / BLOCK), 0.046875, ((1, 128),))
    centers = draw_centers(jax.random.fold_in(arg_keys[7], 71), 0)
    blocks = draw_blocks(jax.random.fold_in(arg_keys[7], 71), 0)
    counts = draw_counts(jax.random.fold_in(arg_keys[7], 71), 0)
    weights = jnp.clip(jnp.exp(math.log(1.0) - 1.609438 * jax.random.uniform(arg_keys[4], (SOURCES,), jnp.float32) ** shard_levels(arg_keys[4], (SOURCES,), ((0, 32),), -0.2, 0.2)), 0.2, 1.0)
    defocus = jnp.clip(jax.random.uniform(arg_keys[5], (CONDS,), jnp.float32, -3.0, 3.0) * shard_levels(arg_keys[5], (CONDS,), ((0, 2),), -0.4, 0.0), -3.0, 3.0)
    dose_scale = jnp.clip(jnp.exp(math.log(2.0) - 1.3862944 * jax.random.uniform(arg_keys[6], (CONDS,), jnp.float32) ** shard_levels(arg_keys[6], (CONDS,), ((0, 2),), -0.2, 0.2)), 0.5, 2.0)
    return {"spectrum": spectrum, "centers": centers, "blocks": blocks, "counts": counts, "weights": weights, "defocus": defocus, "dose_scale": dose_scale}


TAU = 0.5
BACKGROUND = 0.05


def phase_table(first, second, period):
    product = jnp.mod(first[:, None] * second[None, :], period).astype(jnp.float32)
    angle = product * (2.0 * math.pi / period)
    return jnp.cos(angle).astype(jnp.bfloat16), jnp.sin(angle).astype(jnp.bfloat16)


def reference(spectrum, centers, blocks, counts, weights, defocus, dose_scale):
    half_index = SPEC // 2
    spec_index = jnp.arange(SPEC, dtype=jnp.int32)
    image_rows = jnp.arange(X, dtype=jnp.int32)
    columns = jnp.arange(N, dtype=jnp.int32)
    cos_rows, sin_rows = phase_table(image_rows, spec_index - half_index, N)
    cos_cols, sin_cols = phase_table(spec_index - half_index, columns, N)
    spec_re = spectrum[0].astype(jnp.float32)
    spec_im = spectrum[1].astype(jnp.float32)
    offsets = jnp.arange(BLOCK, dtype=jnp.int32)
    slots = jnp.arange(B_MAX, dtype=jnp.int32)

    def per_source(power, item):
        center, listing, count, weight = item

        def per_entry(fields, entry):
            number, slot = entry
            live = (slot < count).astype(jnp.float32)
            row_start = ((number // NB) * BLOCK).astype(jnp.int32)
            col_start = ((number % NB) * BLOCK).astype(jnp.int32)
            block_re = lax.dynamic_slice(spec_re, (row_start, col_start), (BLOCK, BLOCK))
            block_im = lax.dynamic_slice(spec_im, (row_start, col_start), (BLOCK, BLOCK))
            row_gap = (row_start + offsets).astype(jnp.float32) - center[0]
            col_gap = (col_start + offsets).astype(jnp.float32) - center[1]
            radius = (row_gap[:, None] * row_gap[:, None] + col_gap[None, :] * col_gap[None, :]) / (4.0 * BLOCK * BLOCK)
            amplitude = live * jnp.exp(-radius)
            angle = defocus[:, None, None] * radius[None]
            pupil_re = amplitude[None] * jnp.cos(angle)
            pupil_im = amplitude[None] * jnp.sin(angle)
            masked_re = lax.optimization_barrier((block_re * pupil_re - block_im * pupil_im).astype(jnp.bfloat16)).astype(jnp.float32)
            masked_im = lax.optimization_barrier((block_re * pupil_im + block_im * pupil_re).astype(jnp.bfloat16)).astype(jnp.float32)
            row_cos = lax.dynamic_slice_in_dim(cos_rows, row_start, BLOCK, 1).astype(jnp.float32)
            row_sin = lax.dynamic_slice_in_dim(sin_rows, row_start, BLOCK, 1).astype(jnp.float32)
            form = "xa,cab->cxb"
            half_re = jnp.einsum(form, row_cos, masked_re) - jnp.einsum(form, row_sin, masked_im)
            half_im = jnp.einsum(form, row_sin, masked_re) + jnp.einsum(form, row_cos, masked_im)
            half_re = half_re.astype(jnp.bfloat16).reshape(CONDS * X, BLOCK)
            half_im = half_im.astype(jnp.bfloat16).reshape(CONDS * X, BLOCK)
            col_cos = lax.dynamic_slice_in_dim(cos_cols, col_start, BLOCK, 0)
            col_sin = lax.dynamic_slice_in_dim(sin_cols, col_start, BLOCK, 0)
            field_re = fields[0] + jnp.dot(half_re, col_cos, preferred_element_type=jnp.float32) - jnp.dot(half_im, col_sin, preferred_element_type=jnp.float32)
            field_im = fields[1] + jnp.dot(half_re, col_sin, preferred_element_type=jnp.float32) + jnp.dot(half_im, col_cos, preferred_element_type=jnp.float32)
            return (field_re, field_im), None

        start = jnp.zeros((CONDS * X, N), jnp.float32)
        fields, _ = lax.scan(per_entry, (start, start), (listing, slots))
        energy = (fields[0] * fields[0] + fields[1] * fields[1]).reshape(CONDS, X, N)
        return power + weight * energy, None

    power, _ = lax.scan(per_source, jnp.zeros((CONDS, X, N), jnp.float32), (centers, blocks, counts, weights))
    intensity = dose_scale[:, None, None] * power / SOURCES + BACKGROUND
    right = jnp.roll(intensity, -1, axis=2)
    left = jnp.roll(intensity, 1, axis=2)
    slope = jnp.abs(right - left) / (2.0 * intensity)
    terms = jnp.sum(jnp.exp(-slope / TAU), axis=0)
    return -TAU * jnp.log(terms / CONDS)
```

```python
import functools
import math

import jax
import jax.numpy as jnp
from jax import lax
from jax.experimental import pallas as pl
from jax.experimental.pallas import tpu as pltpu
from jax.sharding import PartitionSpec as P

N = 4096
BLOCK = 128
NB = 8
XR = 128
SPEC = 1024
SOURCES = 32
SLOTS = 8
CONDS = 4
W = 32
ROWS = 40

TAU = 0.5
BACKGROUND = 0.05

F32 = jnp.float32
BF16 = jnp.bfloat16

Z_GROUPS = [[z * 4 + y for z in range(8)] for y in range(4)]
Y_GROUPS = [[z * 4 + y for y in range(4)] for z in range(8)]
TILE_GROUPS = [[8 * k + t for k in range(4) for t in (q, 7 - q)] for q in range(4)]


def phases(product):
    angle = jnp.mod(product, N).astype(F32) * (2.0 * math.pi / N)
    return jnp.cos(angle).astype(BF16), jnp.sin(angle).astype(BF16)


def spread(value, axis, groups=None):
    count = 4 if groups is None else len(groups[0])
    copies = jnp.broadcast_to(value[None], (count,) + value.shape)
    return lax.all_to_all(copies, axis, 0, 0, axis_index_groups=groups)


def round_bf16(value):
    return lax.reduce_precision(value, 8, 7)


def kernel(
    counts_ref, slot_ref, i_ref, j_ref, weight_ref, dose_ref,
    own1_ref, own2_ref, oth1_ref, oth2_ref, select_ref,
    p_ref, q_ref, rowf_ref, colf_ref,
    out_ref, turned, pieces, power,
):
    def turn(first, which, x_first):
        ref = (own1_ref, own2_ref, oth1_ref, oth2_ref)[which]

        def body(zi, carry):
            for lane in range(2):
                parts = []
                for n in range(16):
                    y, x = n // 4, n % 4
                    lead = (x, y) if x_first else (y, x)
                    parts.append(ref[lead[0], lead[1], zi, :, 128 * lane:128 * lane + 128].astype(F32))
                stack = jnp.concatenate([p[:8] for p in parts] + [p[8:] for p in parts], axis=0).astype(BF16)
                done = lax.dot_general(
                    select_ref[...], stack, (((1,), (1,)), ((), ())), preferred_element_type=F32
                )
                turned[first + 8 * lane + zi] = done.astype(BF16)
            return carry

        lax.fori_loop(0, 8, body, 0)

    turn(0, 0, True)
    turn(16, 1, False)
    turn(32, 2, True)
    turn(48, 3, False)
    pieces[...] = jnp.zeros_like(pieces)
    power[...] = jnp.zeros_like(power)

    def per_source(s, carry):
        count = counts_ref[s]
        p_all = p_ref[s]
        q_all = jnp.transpose(q_ref[s])

        def entry(k):
            e = s * SLOTS + k
            block = turned[slot_ref[e]].astype(F32)
            re, im = block[:, :128], block[:, 128:]
            pr, pi = p_all[2 * k:2 * k + 1], p_all[2 * k + 1:2 * k + 2]
            qr, qi = q_all[:, 2 * k:2 * k + 1], q_all[:, 2 * k + 1:2 * k + 2]
            pupil_re = qr * pr - qi * pi
            pupil_im = qr * pi + qi * pr
            masked_re = (re * pupil_re - im * pupil_im).astype(BF16)
            masked_im = (re * pupil_im + im * pupil_re).astype(BF16)
            masked = jnp.concatenate([masked_re, masked_im], axis=1)
            piece = jnp.dot(masked, rowf_ref[i_ref[e]], preferred_element_type=F32).astype(BF16)
            for r in range(4):
                pieces[r, 32 * k:32 * k + 32, :] = piece[32 * r:32 * r + 32]

        for pair in range(SLOTS // 2):
            @pl.when(2 * pair < count)
            def _():
                entry(2 * pair)
                entry(2 * pair + 1)

        direct, mirror = [], []
        group = lax.broadcasted_iota(jnp.int32, (2 * ROWS, 128), 1) // 32
        for r in range(4):
            halves = []
            for h in range(2):
                table = None
                for m in range(4):
                    k = 4 * h + m
                    j = jnp.where(k < count, j_ref[s * SLOTS + k], NB)
                    term = colf_ref[j, (m - r) % 4]
                    table = term if table is None else jnp.where(group == m, term, table)
                halves.append(table)
            table = jnp.concatenate(halves, axis=1)
            both = jnp.dot(table, pieces[r], preferred_element_type=F32)
            a_cos, b_cos = both[:ROWS, :128], both[:ROWS, 128:]
            a_sin, b_sin = both[ROWS:, :128], both[ROWS:, 128:]
            direct.append((a_cos - b_sin, a_sin + b_cos))
            mirror.append((a_cos + b_sin, b_cos - a_sin))
        weight = weight_ref[s]
        for base, parts in ((0, direct), (4, mirror)):
            (r0, i0), (r1, i1), (r2, i2), (r3, i3) = parts
            gr, gi, dr, di = r0 + r2, i0 + i2, r0 - r2, i0 - i2
            hr, hi, er, ei = r1 + r3, i1 + i3, r1 - r3, i1 - i3
            images = ((gr + hr, gi + hi), (dr - ei, di + er), (gr - hr, gi - hi), (dr + ei, di - er))
            for m, (fr, fi) in enumerate(images):
                power[base + m] += weight * (fr * fr + fi * fi)
        return carry

    lax.fori_loop(0, SOURCES, per_source, 0)

    dose = dose_ref[0]
    for e in range(8):
        image = e // 2 if e % 2 == 0 else 4 + (e // 2 + 1) % 4
        low = 1 + e % 2
        level = dose * power[image] / SOURCES + BACKGROUND
        slope = jnp.abs(level[low + 1:low + 1 + W] - level[low - 1:low - 1 + W]) / (2.0 * level[low:low + W])
        out_ref[e] = jnp.exp(slope * (-1.0 / TAU))


def on_device(spectrum, centers, blocks, counts, weights, defocus, dose_scale):
    core = lax.axis_index("cond")
    source = lax.axis_index("source")
    z, y = source // 4, source % 4
    half = lax.dynamic_slice(spectrum, (0, 0, 512 * core), (2, 8, 512)).reshape(16, 512)
    info = jnp.concatenate(
        [centers, counts.astype(F32)[:, None], weights[:, None], blocks.astype(F32)], axis=1
    )
    high = round_bf16(info)
    mid = round_bf16(info - high)
    low = round_bf16(info - high - mid)
    info = jnp.concatenate([high, mid, low], axis=0).astype(BF16)
    info = jnp.pad(info, ((0, 13), (0, 116)))
    along_z = spread(jnp.concatenate([half[:, :256], info, half[:, 256:]], axis=1), "source", Z_GROUPS)
    first = spread(along_z[:, :, :384], "source", Y_GROUPS)
    second = spread(along_z[:, :, 384:], "row")
    info = first[:, :, :3, 256:268].astype(F32)
    info = (info[:, :, 0] + info[:, :, 1] + info[:, :, 2]).transpose(1, 0, 2).reshape(SOURCES, 12)
    own1 = spread(first[:, :, :, :256], "row")
    own2 = spread(second, "source", Y_GROUPS)
    swap = [(0, 1), (1, 0)]
    oth1 = lax.ppermute(own1, "cond", swap)
    oth2 = lax.ppermute(own2, "cond", swap)

    all_centers = info[:, :2]
    all_counts = info[:, 2].astype(jnp.int32)
    all_weights = info[:, 3]
    all_blocks = info[:, 4:12].astype(jnp.int32)
    row_block, col_block = all_blocks // NB, all_blocks % NB
    slot = ((col_block // 4) ^ core) * 32 + (col_block % 4) * 8 + row_block
    mine = z % 2
    focus = jnp.where(mine == 0, defocus[0], defocus[1])
    dose = jnp.where(mine == 0, dose_scale[0], dose_scale[1])

    offsets = jnp.arange(BLOCK, dtype=jnp.int32)
    by_residue = (offsets % 32) * 4 + offsets // 32

    def pupil_factor(number, inner, center):
        gap = (number[:, :, None] * BLOCK + inner).astype(F32) - center[:, None, None]
        radius = gap * gap / (4.0 * BLOCK * BLOCK)
        amplitude = jnp.exp(-radius)
        angle = focus * radius
        parts = jnp.stack([amplitude * jnp.cos(angle), amplitude * jnp.sin(angle)], axis=2)
        return parts.reshape(SOURCES, 2 * SLOTS, BLOCK)

    p_all = pupil_factor(row_block, offsets, all_centers[:, 0])
    q_all = pupil_factor(col_block, by_residue, all_centers[:, 1])

    image_rows = lax.axis_index("row") * XR + jnp.arange(XR, dtype=jnp.int32)
    spec_index = jnp.arange(SPEC, dtype=jnp.int32) - SPEC // 2
    row_cos, row_sin = phases(spec_index[:, None] * image_rows[None, :])
    row_cos, row_sin = row_cos.reshape(NB, BLOCK, XR), row_sin.reshape(NB, BLOCK, XR)
    rowf = jnp.concatenate(
        [jnp.concatenate([row_cos, row_sin], axis=2), jnp.concatenate([-row_sin, row_cos], axis=2)], axis=1
    )

    quarter = jnp.where(z % 2 == 0, y, 3 - y)
    window = 4 * quarter + z // 2
    columns = window * W - 1 + jnp.arange(ROWS, dtype=jnp.int32)
    v_index = (jnp.arange(NB, dtype=jnp.int32)[:, None] * BLOCK + by_residue[None, :]) - SPEC // 2
    col_cos, col_sin = phases(v_index[:, None, :] * columns[None, :, None])
    col = jnp.concatenate([col_cos, col_sin], axis=1)
    col = jnp.pad(col, ((0, 1), (0, 0), (0, 0)))
    colf = jnp.stack(
        [col] + [jnp.concatenate([col[:, :, 128 - 32 * d:], col[:, :, :128 - 32 * d]], axis=2) for d in (1, 2, 3)],
        axis=1,
    )
    select = (by_residue[:, None] == offsets[None, :]).astype(BF16)

    vmem = pl.BlockSpec(memory_space=pltpu.VMEM)
    smem = pl.BlockSpec(memory_space=pltpu.SMEM)
    terms = pl.pallas_call(
        kernel,
        out_shape=jax.ShapeDtypeStruct((8, W, XR), F32),
        in_specs=[smem] * 6 + [vmem] * 9,
        out_specs=vmem,
        scratch_shapes=[
            pltpu.VMEM((64, 128, 256), BF16),
            pltpu.VMEM((4, 256, 256), BF16),
            pltpu.VMEM((8, ROWS, XR), F32),
        ],
        compiler_params=pltpu.CompilerParams(vmem_limit_bytes=40 * 1024 * 1024),
    )(
        all_counts, slot.reshape(-1), row_block.reshape(-1), col_block.reshape(-1), all_weights, dose.reshape(1),
        own1, own2, oth1, oth2, select, p_all, q_all, rowf, colf,
    )
    terms = lax.all_to_all(terms, "source", 0, 0, axis_index_groups=TILE_GROUPS)
    terms = terms.reshape(4, 2, W, XR)
    terms = (terms[:, 0] + terms[:, 1]).reshape(4 * W, XR)
    total = terms + lax.ppermute(terms, "cond", swap)
    soft = -TAU * jnp.log(total / CONDS)
    soft = jnp.where(z % 2 == 0, soft, soft[::-1])
    return soft.T


def solution(mesh):
    in_specs = (
        P(None, ("source", "row"), None),
        P("source", None),
        P("source", None),
        P("source"),
        P("source"),
        P("cond"),
        P("cond"),
    )
    out_specs = P("row", "source")
    return jax.shard_map(
        on_device, mesh=mesh, in_specs=in_specs, out_specs=out_specs, check_vma=False
    )
```

```python
import functools
import math

import jax
import jax.numpy as jnp
from jax import lax
from jax.experimental import pallas as pl
from jax.experimental.pallas import tpu as pltpu
from jax.sharding import PartitionSpec as P

N = 4096
BLOCK = 128
NB = 8
XR = 128
SPEC = 1024
SOURCES = 32
SLOTS = 8
CONDS = 4
W = 64
ROWS = 72
PART = 32
PART_ROWS = 40
GROUP = 4
LOCAL = SOURCES // 2
ENTRIES = LOCAL * SLOTS

TAU = 0.5
BACKGROUND = 0.05

F32 = jnp.float32
BF16 = jnp.bfloat16

TILE_GROUPS = [[8 * k + t for k in range(4) for t in (q, 7 - q)] for q in range(4)]


def phases(product):
    angle = jnp.mod(product, N).astype(F32) * (2.0 * math.pi / N)
    return jnp.cos(angle).astype(BF16), jnp.sin(angle).astype(BF16)


def spread(value, axis, count):
    copies = jnp.broadcast_to(value[None], (count,) + value.shape)
    return lax.all_to_all(copies, axis, 0, 0)


def round_bf16(value):
    return lax.reduce_precision(value, 8, 7)


def turn_kernel(rows_ref, select_ref, out_ref):
    for j in range(4):
        parts = [
            rows_ref[n % 4, n // 4, :, 128 * j:128 * j + 128].astype(F32) for n in range(16)
        ]
        stack = jnp.concatenate([p[:8] for p in parts] + [p[8:] for p in parts], axis=0).astype(BF16)
        done = lax.dot_general(
            select_ref[...], stack, (((1,), (1,)), ((), ())), preferred_element_type=F32
        )
        out_ref[0, j] = done.astype(BF16)


def image_kernel(
    total_ref, home_ref, slot_ref, block_ref, i_ref, j_ref, weight_ref, core_ref,
    own_ref, other_ref, p_ref, q_ref, rowf_ref, colf_ref,
    keep_ref, send_ref, turned, pieces, power, sems,
):
    copies = [
        pltpu.make_async_copy(ref, turned.at[pl.ds(32 * n, 32)], sems.at[n])
        for n, ref in enumerate((own_ref, other_ref))
    ]
    for copy in copies:
        copy.start()
    pieces[...] = jnp.zeros_like(pieces)
    power[...] = jnp.zeros_like(power)
    for copy in copies:
        copy.wait()

    def entries(g, carry):
        p_all = p_ref[g]
        q_all = jnp.transpose(q_ref[g])
        for n in range(GROUP):
            t = g * GROUP + n
            block = turned[block_ref[t]].astype(F32)
            re, im = block[:, :128], block[:, 128:]
            pr, pi = p_all[2 * n:2 * n + 1], p_all[2 * n + 1:2 * n + 2]
            qr, qi = q_all[:, 2 * n:2 * n + 1], q_all[:, 2 * n + 1:2 * n + 2]
            pupil_re = qr * pr - qi * pi
            pupil_im = qr * pi + qi * pr
            masked_re = (re * pupil_re - im * pupil_im).astype(BF16)
            masked_im = (re * pupil_im + im * pupil_re).astype(BF16)
            masked = jnp.concatenate([masked_re, masked_im], axis=1)
            piece = jnp.dot(masked, rowf_ref[i_ref[t]], preferred_element_type=F32).astype(BF16)
            place = pl.ds(pl.multiple_of(32 * slot_ref[t], 32), 32)
            for r in range(4):
                pieces[home_ref[t], r, place, :] = piece[32 * r:32 * r + 32]
        return carry

    lax.fori_loop(0, (total_ref[0] + GROUP - 1) // GROUP, entries, 0)

    lane_group = lax.broadcasted_iota(jnp.int32, (2 * ROWS, 128), 1) // 32

    def fields(s, carry):
        direct, mirror = [], []
        for r in range(4):
            halves = []
            for h in range(2):
                table = None
                for m in range(4):
                    term = colf_ref[j_ref[s * SLOTS + 4 * h + m], (m - r) % 4]
                    table = term if table is None else jnp.where(lane_group == m, term, table)
                halves.append(table)
            table = jnp.concatenate(halves, axis=1)
            both = jnp.dot(table, pieces[s, r], preferred_element_type=F32)
            a_cos, b_cos = both[:ROWS, :128], both[:ROWS, 128:]
            a_sin, b_sin = both[ROWS:, :128], both[ROWS:, 128:]
            direct.append((a_cos - b_sin, a_sin + b_cos))
            mirror.append((a_cos + b_sin, b_cos - a_sin))
        weight = weight_ref[s]
        for base, parts in ((0, direct), (4, mirror)):
            (r0, i0), (r1, i1), (r2, i2), (r3, i3) = parts
            gr, gi, dr, di = r0 + r2, i0 + i2, r0 - r2, i0 - i2
            hr, hi, er, ei = r1 + r3, i1 + i3, r1 - r3, i1 - i3
            images = ((gr + hr, gi + hi), (dr - ei, di + er), (gr - hr, gi - hi), (dr + ei, di - er))
            for m, (fr, fi) in enumerate(images):
                power[base + m] += weight * (fr * fr + fi * fi)
        return carry

    lax.fori_loop(0, LOCAL, fields, 0)
    mine = pl.multiple_of(PART * core_ref[0], PART)
    theirs = pl.multiple_of(PART * (1 - core_ref[0]), PART)
    for image in range(8):
        keep_ref[image] = power[image, pl.ds(mine, PART_ROWS), :]
        send_ref[image] = power[image, pl.ds(theirs, PART_ROWS), :]


def slope_kernel(dose_ref, keep_ref, other_ref, out_ref):
    dose = dose_ref[0]
    for e in range(8):
        image = e // 2 if e % 2 == 0 else 4 + (e // 2 + 1) % 4
        low = 1 + e % 2
        level = dose * (keep_ref[image] + other_ref[image]) / SOURCES + BACKGROUND
        slope = jnp.abs(level[low + 1:low + 1 + PART] - level[low - 1:low - 1 + PART]) / (
            2.0 * level[low:low + PART]
        )
        out_ref[e] = jnp.exp(slope * (-1.0 / TAU))


def on_device(spectrum, centers, blocks, counts, weights, defocus, dose_scale):
    core = lax.axis_index("cond")
    source = lax.axis_index("source")
    z, y = source // 4, source % 4
    swap = [(0, 1), (1, 0)]
    half = lax.dynamic_slice(spectrum, (0, 0, 512 * core), (2, 8, 512)).reshape(16, 512)
    info = jnp.concatenate(
        [centers, counts.astype(F32)[:, None], weights[:, None], blocks.astype(F32)], axis=1
    )
    high = round_bf16(info)
    mid = round_bf16(info - high)
    low = round_bf16(info - high - mid)
    info = jnp.concatenate([high, mid, low], axis=0).astype(BF16)
    info = jnp.pad(info, ((0, 13), (0, 116)))
    column = spread(jnp.concatenate([half, info], axis=1), "source", 32)
    rows = spread(column[:, :, :512], "row", 4)

    local = jnp.concatenate([defocus, dose_scale])
    remote = lax.ppermute(local, "cond", swap)
    cond = z % 4
    chosen = jnp.where(cond // 2 == core, local, remote)
    focus = jnp.where(cond % 2 == 0, chosen[0], chosen[1])
    dose = jnp.where(cond % 2 == 0, chosen[2], chosen[3])
    quarter = jnp.where(z % 2 == 0, y, 3 - y)
    window = 2 * quarter + z // 4

    info = column[:, :3, 512:524].astype(F32)
    info = info[:, 0] + info[:, 1] + info[:, 2]
    number = jnp.arange(SOURCES, dtype=jnp.int32)
    used = info[:, 2]
    before = (used[None, :] > used[:, None]) | (
        (used[None, :] == used[:, None]) & (number[None, :] < number[:, None])
    )
    rank = jnp.sum(before.astype(jnp.int32), axis=1)
    position = jnp.arange(LOCAL, dtype=jnp.int32)
    wanted = 4 * (position // 2) + jnp.where(position % 2 == 0, core, 3 - core)
    picked = jnp.where(rank[None, :, None] == wanted[:, None, None], info[None], 0.0)
    info = jnp.sum(picked, axis=1)
    used = info[:, 2].astype(jnp.int32)
    listing = info[:, 4:12].astype(jnp.int32)
    start = jnp.sum(jnp.where(position[None, :] < position[:, None], used[None, :], 0), axis=1)
    total = jnp.sum(used)
    entry = jnp.arange(ENTRIES, dtype=jnp.int32)
    inside = (entry[:, None] >= start[None, :]) & (entry[:, None] < (start + used)[None, :])
    home = LOCAL - jnp.sum(jnp.where(inside, LOCAL - position[None, :], 0), axis=1)
    slot = jnp.sum(jnp.where(inside, entry[:, None] - start[None, :], 0), axis=1)
    center = jnp.sum(jnp.where(inside[:, :, None], info[None, :, :2], 0.0), axis=1)
    slots = jnp.arange(SLOTS, dtype=jnp.int32)
    chosen = inside[:, :, None] & (slots[None, None, :] == slot[:, None, None])
    number = jnp.sum(jnp.where(chosen, listing[None], 0), axis=(1, 2))
    row_block, col_block = number // NB, number % NB
    block = ((col_block // 4) ^ core) * 32 + row_block * 4 + col_block % 4
    col_list = jnp.where(slots[None, :] < used[:, None], listing % NB, NB)

    offsets = jnp.arange(BLOCK, dtype=jnp.int32)
    by_residue = (offsets % 32) * 4 + offsets // 32

    def pupil_factor(number, inner, center):
        gap = (number[:, None] * BLOCK + inner[None, :]).astype(F32) - center[:, None]
        radius = gap * gap / (4.0 * BLOCK * BLOCK)
        amplitude = jnp.exp(-radius)
        angle = focus * radius
        parts = jnp.stack([amplitude * jnp.cos(angle), amplitude * jnp.sin(angle)], axis=1)
        return parts.reshape(ENTRIES // GROUP, 2 * GROUP, BLOCK)

    p_all = pupil_factor(row_block, offsets, center[:, 0])
    q_all = pupil_factor(col_block, by_residue, center[:, 1])

    image_rows = lax.axis_index("row") * XR + jnp.arange(XR, dtype=jnp.int32)
    spec_index = jnp.arange(SPEC, dtype=jnp.int32) - SPEC // 2
    row_cos, row_sin = phases(spec_index[:, None] * image_rows[None, :])
    row_cos, row_sin = row_cos.reshape(NB, BLOCK, XR), row_sin.reshape(NB, BLOCK, XR)
    rowf = jnp.concatenate(
        [jnp.concatenate([row_cos, row_sin], axis=2), jnp.concatenate([-row_sin, row_cos], axis=2)], axis=1
    )

    columns = window * W - 1 + jnp.arange(ROWS, dtype=jnp.int32)
    v_index = (jnp.arange(NB, dtype=jnp.int32)[:, None] * BLOCK + by_residue[None, :]) - SPEC // 2
    col_cos, col_sin = phases(v_index[:, None, :] * columns[None, :, None])
    col = jnp.concatenate([col_cos, col_sin], axis=1)
    col = jnp.pad(col, ((0, 1), (0, 0), (0, 0)))
    colf = jnp.stack(
        [col] + [jnp.concatenate([col[:, :, 128 - 32 * d:], col[:, :, :128 - 32 * d]], axis=2) for d in (1, 2, 3)],
        axis=1,
    )
    select = (by_residue[:, None] == offsets[None, :]).astype(BF16)

    own = pl.pallas_call(
        turn_kernel,
        grid=(8,),
        out_shape=jax.ShapeDtypeStruct((8, 4, 128, 256), BF16),
        in_specs=[
            pl.BlockSpec((4, 4, 16, 512), lambda i: (0, i, 0, 0)),
            pl.BlockSpec((128, 128), lambda i: (0, 0)),
        ],
        out_specs=pl.BlockSpec((1, 4, 128, 256), lambda i: (i, 0, 0, 0)),
    )(rows, select)
    own = own.reshape(32, 128, 256)
    other = lax.ppermute(own, "cond", swap)

    vmem = pl.BlockSpec(memory_space=pltpu.VMEM)
    smem = pl.BlockSpec(memory_space=pltpu.SMEM)
    hbm = pl.BlockSpec(memory_space=pl.ANY)
    keep, send = pl.pallas_call(
        image_kernel,
        out_shape=[jax.ShapeDtypeStruct((8, PART_ROWS, XR), F32)] * 2,
        in_specs=[smem] * 8 + [hbm] * 2 + [vmem] * 4,
        out_specs=[vmem] * 2,
        scratch_shapes=[
            pltpu.VMEM((64, 128, 256), BF16),
            pltpu.VMEM((LOCAL + 1, 4, 256, 256), BF16),
            pltpu.VMEM((8, ROWS, XR), F32),
            pltpu.SemaphoreType.DMA((2,)),
        ],
        compiler_params=pltpu.CompilerParams(vmem_limit_bytes=40 * 1024 * 1024),
    )(
        total.reshape(1), home, slot, block, row_block, col_list.reshape(-1), info[:, 3], core.reshape(1),
        own, other, p_all, q_all, rowf, colf,
    )
    received = lax.ppermute(send, "cond", swap)
    terms = pl.pallas_call(
        slope_kernel,
        out_shape=jax.ShapeDtypeStruct((8, PART, XR), F32),
        in_specs=[smem, vmem, vmem],
        out_specs=vmem,
    )(dose.reshape(1), keep, received)
    terms = lax.all_to_all(terms, "source", 0, 0, axis_index_groups=TILE_GROUPS)
    soft = -TAU * jnp.log(jnp.sum(terms.reshape(2, CONDS, PART, XR), axis=1) / CONDS)
    theirs = lax.ppermute(soft, "cond", swap)
    first, second = jnp.where(core == 0, soft, theirs), jnp.where(core == 0, theirs, soft)
    soft = jnp.stack([first, second], axis=1).reshape(2 * W, XR)
    soft = jnp.where(z % 2 == 0, soft, soft[::-1])
    return soft.T


def solution(mesh):
    in_specs = (
        P(None, ("source", "row"), None),
        P("source", None),
        P("source", None),
        P("source"),
        P("source"),
        P("cond"),
        P("cond"),
    )
    out_specs = P("row", "source")
    return jax.shard_map(
        on_device, mesh=mesh, in_specs=in_specs, out_specs=out_specs, check_vma=False
    )
```

```python
import functools
import math

import jax
import jax.numpy as jnp
from jax import lax
from jax.experimental import pallas as pl
from jax.experimental.pallas import tpu as pltpu
from jax.sharding import PartitionSpec as P

N = 4096
BLOCK = 128
NB = 8
XR = 128
SPEC = 1024
SOURCES = 32
SLOTS = 8
CONDS = 4
W = 64
ROWS = 72
PART = 32
PART_ROWS = 40
GROUP = 16
LOCAL = SOURCES // 2
ENTRIES = LOCAL * SLOTS

TAU = 0.5
BACKGROUND = 0.05

MIB = 1024 * 1024
F32 = jnp.float32
BF16 = jnp.bfloat16

Z_GROUPS = [[z * 4 + y for z in range(8)] for y in range(4)]
PLANE_GROUPS = [[z * 16 + n for n in range(16)] for z in range(8)]
TILE_GROUPS = [[8 * k + t for k in range(4) for t in (q, 7 - q)] for q in range(4)]


def turn_by(angle, quarter):
    square = angle * angle
    sine = 1.0 + square * (-1.0 / 6.0 + square * (1.0 / 120.0 + square * (-1.0 / 5040.0 + square * (1.0 / 362880.0))))
    sine = angle * sine
    cosine = 1.0 + square * (-0.5 + square * (1.0 / 24.0 + square * (-1.0 / 720.0 + square * (1.0 / 40320.0))))
    odd = (quarter & 1) == 1
    first, second = jnp.where(odd, sine, cosine), jnp.where(odd, cosine, sine)
    cosine = jnp.where(((quarter + 1) & 2) == 2, -first, first)
    sine = jnp.where((quarter & 2) == 2, -second, second)
    return cosine, sine


def phases(product):
    turn = product & (N - 1)
    quarter = (turn + N // 8) >> 10
    return turn_by((turn - (quarter << 10)).astype(F32) * (2.0 * math.pi / N), quarter)


def pupil_factor(gap, focus):
    radius = gap * gap * (1.0 / (4.0 * BLOCK * BLOCK))
    amplitude = jnp.exp(-radius)
    angle = focus * radius
    quarter = jnp.floor(angle * (2.0 / math.pi) + 0.5)
    angle = angle - quarter * 1.5703125
    angle = angle - quarter * 4.837512969970703e-4
    angle = angle - quarter * 7.549789954891882e-8
    cosine, sine = turn_by(angle, quarter.astype(jnp.int32))
    return amplitude * cosine, amplitude * sine


def table_kernel(place_ref, rowf_ref, colf_ref):
    first_row, first_column = place_ref[0], place_ref[1]
    u = lax.broadcasted_iota(jnp.int32, (BLOCK, XR), 0) - SPEC // 2
    x = lax.broadcasted_iota(jnp.int32, (BLOCK, XR), 1) + first_row
    y = lax.broadcasted_iota(jnp.int32, (ROWS, BLOCK), 0) + first_column
    lane = lax.broadcasted_iota(jnp.int32, (ROWS, BLOCK), 1)
    v = (lane & 31) * 4 + (lane >> 5) - SPEC // 2

    def body(n, carry):
        cosine, sine = phases((u + n * BLOCK) * x)
        cosine, sine, minus = cosine.astype(BF16), sine.astype(BF16), (-sine).astype(BF16)
        rowf_ref[n, :BLOCK, :XR] = cosine
        rowf_ref[n, :BLOCK, XR:] = sine
        rowf_ref[n, BLOCK:, :XR] = minus
        rowf_ref[n, BLOCK:, XR:] = cosine
        both = jnp.concatenate(phases((v + n * BLOCK) * y), axis=0)
        colf_ref[n, 0] = both.astype(BF16)
        for d in (1, 2, 3):
            colf_ref[n, d] = pltpu.roll(both, 32 * d, 1).astype(BF16)
        return carry

    lax.fori_loop(0, NB, body, 0)
    colf_ref[NB] = jnp.zeros((4, 2 * ROWS, BLOCK), BF16)


def round_bf16(value):
    return value.astype(BF16).astype(F32)


def pack_kernel(core_ref, centers_ref, counts_ref, weights_ref, blocks_ref, spectrum_ref, out_ref):
    start = pl.multiple_of(512 * core_ref[0], 512)
    half = spectrum_ref[:, :, pl.ds(start, 512)].astype(F32).reshape(16, 512).astype(BF16)
    rows = lax.broadcasted_iota(jnp.int32, (BLOCK, BLOCK), 0)
    lanes = lax.broadcasted_iota(jnp.int32, (BLOCK, BLOCK), 1)
    select = (rows == (lanes & 31) * 4 + (lanes >> 5)).astype(F32).astype(BF16)
    parts = [
        jnp.dot(half[:, 128 * j:128 * j + 128], select, preferred_element_type=F32).astype(BF16)
        for j in range(4)
    ]
    numbers = [centers_ref[0, 0], centers_ref[0, 1], counts_ref[0, 0].astype(F32), weights_ref[0, 0]]
    numbers += [blocks_ref[0, k].astype(F32) for k in range(SLOTS)]
    lane = lax.broadcasted_iota(jnp.int32, (16, 128), 1)
    info = jnp.zeros((16, 128), F32)
    for n, value in enumerate(numbers):
        info = jnp.where(lane & 15 == n, value, info)
    high = round_bf16(info)
    mid = round_bf16(info - high)
    low = info - high - mid
    info = jnp.where(lane < 16, high, jnp.where(lane < 32, mid, low)).astype(BF16)
    for n in range(8):
        for j in range(4):
            out_ref[n, j] = parts[j]
        out_ref[n, 4] = info


def spread_kernel(column_ref, out_ref):
    row = lax.broadcasted_iota(jnp.int32, (16, 128), 0)
    info = jnp.zeros((16, 128), F32)
    for n in range(8):
        info = jnp.where(row == n, column_ref[n, 4].astype(F32)[0:1], info)
    info = info.astype(BF16)
    for m in range(16):
        for n in range(8):
            out_ref[m, 4 * n:4 * n + 4] = column_ref[n, :4]
        out_ref[m, 32] = info


def turn_kernel(rows_ref, out_ref):
    for i in range(2):
        for j in range(4):
            parts = [rows_ref[n, 4 * i + j].astype(F32) for n in range(16)]
            stack = jnp.concatenate([p[:8] for p in parts] + [p[8:] for p in parts], axis=0)
            out_ref[i, j] = jnp.transpose(stack.astype(BF16))


def image_kernel(
    info_ref, whole_ref, focus_ref, core_ref, own_ref, other_ref, rowf_ref, colf_ref,
    keep_ref, send_ref, turned, pieces, power, even, odd, numbers, p_re, p_im, q_re, q_im, listing, sems,
):
    def count_of(s):
        return whole_ref[16 * s + 2]

    def block_of(e):
        return whole_ref[((e >> 3) << 4) + 4 + (e & 7)]

    copies = [
        pltpu.make_async_copy(ref, turned.at[pl.ds(32 * n, 32)], sems.at[n])
        for n, ref in enumerate((own_ref, other_ref))
    ]
    for copy in copies:
        copy.start()

    def live(s, total):
        for k in range(SLOTS):
            listing[total + k] = s * SLOTS + k
        return total + count_of(s)

    total = lax.fori_loop(0, LOCAL, live, 0)
    for n in range(GROUP):
        listing[total + n] = ENTRIES
    groups = (total + GROUP - 1) >> 4
    lane = lax.broadcasted_iota(jnp.int32, (SLOTS, BLOCK), 1)
    by_residue = ((lane & 31) * 4 + (lane >> 5)).astype(F32)
    lane = lane.astype(F32)
    for s in range(LOCAL):
        rows = slice(SLOTS * s, SLOTS * s + SLOTS)
        for k in range(SLOTS):
            numbers[SLOTS * s + k:SLOTS * s + k + 1, :] = jnp.full((1, BLOCK), info_ref[16 * s + 4 + k])
        number = numbers[rows, :]
        i = jnp.floor(number * (1.0 / NB))
        j = number - i * NB
        p_re[rows, :], p_im[rows, :] = pupil_factor(i * BLOCK + lane - info_ref[16 * s], focus_ref[0])
        q_re[rows, :], q_im[rows, :] = pupil_factor(j * BLOCK + by_residue - info_ref[16 * s + 1], focus_ref[0])

    pieces[...] = jnp.zeros_like(pieces)
    power[...] = jnp.zeros_like(power)
    for copy in copies:
        copy.wait()

    def entries(g, carry):
        places = [listing[g * GROUP + n] for n in range(GROUP)]
        sources = [jnp.minimum(e, ENTRIES - 1) for e in places]
        q_all = jnp.transpose(
            jnp.concatenate([part[pl.ds(e, 1), :] for part in (q_re, q_im) for e in sources], axis=0)
        )
        for n in range(GROUP):
            number = block_of(sources[n])
            i, j = number >> 3, number & 7
            block = turned[(((j >> 2) ^ core_ref[0]) << 5) + (i << 2) + (j & 3)].astype(F32)
            re, im = block[:, :128], block[:, 128:]
            pr, pi = p_re[pl.ds(sources[n], 1), :], p_im[pl.ds(sources[n], 1), :]
            qr, qi = q_all[:, n:n + 1], q_all[:, GROUP + n:GROUP + n + 1]
            pupil_re = qr * pr - qi * pi
            pupil_im = qr * pi + qi * pr
            masked_re = (re * pupil_re - im * pupil_im).astype(BF16)
            masked_im = (re * pupil_im + im * pupil_re).astype(BF16)
            masked = jnp.concatenate([masked_re, masked_im], axis=1)
            piece = jnp.dot(masked, rowf_ref[i], preferred_element_type=F32).astype(BF16)
            place = pl.ds(pl.multiple_of(32 * (places[n] & 7), 32), 32)
            for r in range(4):
                pieces[places[n] >> 3, r, place, :] = piece[32 * r:32 * r + 32]
        return carry

    lax.fori_loop(0, groups, entries, 0)

    lane_group = lax.broadcasted_iota(jnp.int32, (2 * ROWS, 128), 1) // 32

    def transform(s, buffer):
        columns = [
            jnp.where(k < count_of(s), whole_ref[16 * s + 4 + k] & 7, NB) for k in range(SLOTS)
        ]
        for r in range(4):
            halves = []
            for h in range(2):
                table = None
                for m in range(4):
                    term = colf_ref[columns[4 * h + m], (m - r) % 4]
                    table = term if table is None else jnp.where(lane_group == m, term, table)
                halves.append(table)
            table = jnp.concatenate(halves, axis=1)
            buffer[r] = jnp.dot(table, pieces[s, r], preferred_element_type=F32)

    def gather_power(s, buffer):
        weight = info_ref[16 * s + 3]
        for c in range(ROWS // 8):
            low = slice(8 * c, 8 * c + 8)
            high = slice(ROWS + 8 * c, ROWS + 8 * c + 8)
            direct, mirror = [], []
            for r in range(4):
                a_cos, b_cos = buffer[r, low, :128], buffer[r, low, 128:]
                a_sin, b_sin = buffer[r, high, :128], buffer[r, high, 128:]
                direct.append((a_cos - b_sin, a_sin + b_cos))
                mirror.append((a_cos + b_sin, b_cos - a_sin))
            for base, parts in ((0, direct), (4, mirror)):
                (r0, i0), (r1, i1), (r2, i2), (r3, i3) = parts
                gr, gi, dr, di = r0 + r2, i0 + i2, r0 - r2, i0 - i2
                hr, hi, er, ei = r1 + r3, i1 + i3, r1 - r3, i1 - i3
                images = ((gr + hr, gi + hi), (dr - ei, di + er), (gr - hr, gi - hi), (dr + ei, di - er))
                for m, (fr, fi) in enumerate(images):
                    power[base + m, low] += weight * (fr * fr + fi * fi)

    transform(0, even)
    def two(i, carry):
        gather_power(2 * i, even)
        transform(2 * i + 1, odd)
        gather_power(2 * i + 1, odd)
        transform(jnp.minimum(2 * i + 2, LOCAL - 1), even)
        return carry
    lax.fori_loop(0, LOCAL // 2, two, 0)
    mine = pl.multiple_of(PART * core_ref[0], PART)
    theirs = pl.multiple_of(PART * (1 - core_ref[0]), PART)
    for image in range(8):
        keep_ref[image] = power[image, pl.ds(mine, PART_ROWS), :]
        send_ref[image] = power[image, pl.ds(theirs, PART_ROWS), :]


def slope_kernel(dose_ref, keep_ref, other_ref, out_ref):
    dose = dose_ref[0]
    for e in range(8):
        image = e // 2 if e % 2 == 0 else 4 + (e // 2 + 1) % 4
        low = 1 + e % 2
        level = dose * (keep_ref[image] + other_ref[image]) / SOURCES + BACKGROUND
        slope = jnp.abs(level[low + 1:low + 1 + PART] - level[low - 1:low - 1 + PART]) / (
            2.0 * level[low:low + PART]
        )
        out_ref[e] = jnp.exp(slope * (-1.0 / TAU))


def on_device(spectrum, centers, blocks, counts, weights, defocus, dose_scale):
    core = lax.axis_index("cond")
    source = lax.axis_index("source")
    z, y = source // 4, source % 4
    swap = [(0, 1), (1, 0)]
    vmem = pl.BlockSpec(memory_space=pltpu.VMEM)
    smem = pl.BlockSpec(memory_space=pltpu.SMEM)
    hbm = pl.BlockSpec(memory_space=pl.ANY)
    packed = pl.pallas_call(
        pack_kernel,
        out_shape=jax.ShapeDtypeStruct((8, 5, 16, 128), BF16),
        in_specs=[smem] * 5 + [vmem],
        out_specs=vmem,
        compiler_params=pltpu.CompilerParams(vmem_limit_bytes=56 * MIB),
    )(core.reshape(1), centers, counts.reshape(1, 1), weights.reshape(1, 1), blocks, spectrum)
    defocus, dose_scale, packed = lax.optimization_barrier((defocus, dose_scale, packed))

    local = jnp.concatenate([defocus, dose_scale])
    remote = lax.ppermute(local, "cond", swap)
    cond = z % 4
    chosen = jnp.where(cond // 2 == core, local, remote)
    focus = jnp.where(cond % 2 == 0, chosen[0], chosen[1])
    dose = jnp.where(cond % 2 == 0, chosen[2], chosen[3])
    quarter = jnp.where(z % 2 == 0, y, 3 - y)
    window = 2 * quarter + z // 4
    place = jnp.stack([lax.axis_index("row") * XR, window * W - 1])
    place, packed = lax.optimization_barrier((place, packed))
    rowf, colf = pl.pallas_call(
        table_kernel,
        out_shape=[
            jax.ShapeDtypeStruct((NB, 2 * BLOCK, 2 * XR), BF16),
            jax.ShapeDtypeStruct((NB + 1, 4, 2 * ROWS, BLOCK), BF16),
        ],
        in_specs=[smem],
        out_specs=[vmem, vmem],
        compiler_params=pltpu.CompilerParams(vmem_limit_bytes=8 * MIB),
    )(place)

    column = lax.all_to_all(packed, "source", 0, 0, axis_index_groups=Z_GROUPS)
    copies = pl.pallas_call(
        spread_kernel,
        out_shape=jax.ShapeDtypeStruct((16, 33, 16, 128), BF16),
        in_specs=[vmem],
        out_specs=vmem,
        compiler_params=pltpu.CompilerParams(vmem_limit_bytes=4 * MIB),
    )(column)
    rows = lax.all_to_all(copies, ("source", "row"), 0, 0, axis_index_groups=PLANE_GROUPS)
    rows, rowf, colf, dose, focus = lax.optimization_barrier((rows, rowf, colf, dose, focus))
    own = pl.pallas_call(
        turn_kernel,
        grid=(4,),
        out_shape=jax.ShapeDtypeStruct((8, 4, 128, 256), BF16),
        in_specs=[pl.BlockSpec((16, 8, 16, 128), lambda i: (0, i, 0, 0))],
        out_specs=pl.BlockSpec((2, 4, 128, 256), lambda i: (i, 0, 0, 0)),
        compiler_params=pltpu.CompilerParams(vmem_limit_bytes=8 * MIB),
    )(rows)
    own = own.reshape(32, 128, 256)
    other = lax.ppermute(own, "cond", swap)

    info = lax.dynamic_slice(rows, (8 * core, 32, 0, 0), (8, 1, 8, 48))[::4, 0].astype(F32)
    info = (info[:, :, :16] + info[:, :, 16:32] + info[:, :, 32:]).reshape(-1)
    keep, send = pl.pallas_call(
        image_kernel,
        out_shape=[jax.ShapeDtypeStruct((8, PART_ROWS, XR), F32)] * 2,
        in_specs=[smem] * 4 + [hbm] * 2 + [vmem] * 2,
        out_specs=[vmem] * 2,
        scratch_shapes=[
            pltpu.VMEM((64, 128, 256), BF16),
            pltpu.VMEM((LOCAL + 1, 4, 256, 256), BF16),
            pltpu.VMEM((8, ROWS, XR), F32),
            pltpu.VMEM((4, 2 * ROWS, 256), F32),
            pltpu.VMEM((4, 2 * ROWS, 256), F32),
        ] + [pltpu.VMEM((ENTRIES, BLOCK), F32)] * 5 + [
            pltpu.SMEM((ENTRIES + GROUP,), jnp.int32),
            pltpu.SemaphoreType.DMA((2,)),
        ],
        compiler_params=pltpu.CompilerParams(vmem_limit_bytes=24 * MIB),
    )(info, info.astype(jnp.int32), focus.reshape(1), core.reshape(1), own, other, rowf, colf)
    received = lax.ppermute(send, "cond", swap)
    terms = pl.pallas_call(
        slope_kernel,
        out_shape=jax.ShapeDtypeStruct((8, PART, XR), F32),
        in_specs=[smem, vmem, vmem],
        out_specs=vmem,
        compiler_params=pltpu.CompilerParams(vmem_limit_bytes=4 * MIB),
    )(dose.reshape(1), keep, received)
    terms = lax.all_to_all(terms, "source", 0, 0, axis_index_groups=TILE_GROUPS)
    soft = -TAU * jnp.log(jnp.sum(terms.reshape(2, CONDS, PART, XR), axis=1) / CONDS)
    theirs = lax.ppermute(soft, "cond", swap)
    first, second = jnp.where(core == 0, soft, theirs), jnp.where(core == 0, theirs, soft)
    soft = jnp.stack([first, second], axis=1).reshape(2 * W, XR)
    soft = jnp.where(z % 2 == 0, soft, soft[::-1])
    return soft.T


def solution(mesh):
    in_specs = (
        P(None, ("source", "row"), None),
        P("source", None),
        P("source", None),
        P("source"),
        P("source"),
        P("cond"),
        P("cond"),
    )
    out_specs = P("row", "source")
    return jax.shard_map(
        on_device, mesh=mesh, in_specs=in_specs, out_specs=out_specs, check_vma=False
    )
```

```python
import functools
import math

import jax
import jax.numpy as jnp
from jax import lax
from jax.experimental import pallas as pl
from jax.experimental.pallas import tpu as pltpu
from jax.sharding import PartitionSpec as P

N = 4096
BLOCK = 128
NB = 8
XR = 128
SPEC = 1024
SOURCES = 32
SLOTS = 8
CONDS = 4
W = 64
ROWS = 72
PART = 32
PART_ROWS = 40
GROUP = 16
LOCAL = SOURCES // 2
ENTRIES = LOCAL * SLOTS

TAU = 0.5
BACKGROUND = 0.05

MIB = 1024 * 1024
F32 = jnp.float32
BF16 = jnp.bfloat16

Z_GROUPS = [[z * 4 + y for z in range(8)] for y in range(4)]
X_LINES = [[[((z * 4 + y) * 4 + x) * 2 + c for x in range(4)] for z in range(8) for y in range(4)] for c in range(2)]
Y_LINES = [[[((z * 4 + y) * 4 + x) * 2 + c for y in range(4)] for z in range(8) for x in range(4)] for c in range(2)]
TILE_GROUPS = [[8 * k + t for k in range(4) for t in (q, 7 - q)] for q in range(4)]


def turn_by(angle, quarter):
    square = angle * angle
    sine = 1.0 + square * (-1.0 / 6.0 + square * (1.0 / 120.0 + square * (-1.0 / 5040.0 + square * (1.0 / 362880.0))))
    sine = angle * sine
    cosine = 1.0 + square * (-0.5 + square * (1.0 / 24.0 + square * (-1.0 / 720.0 + square * (1.0 / 40320.0))))
    odd = (quarter & 1) == 1
    first, second = jnp.where(odd, sine, cosine), jnp.where(odd, cosine, sine)
    cosine = jnp.where(((quarter + 1) & 2) == 2, -first, first)
    sine = jnp.where((quarter & 2) == 2, -second, second)
    return cosine, sine


def phases(product):
    turn = product & (N - 1)
    quarter = (turn + N // 8) >> 10
    return turn_by((turn - (quarter << 10)).astype(F32) * (2.0 * math.pi / N), quarter)


def pupil_factor(gap, focus):
    radius = gap * gap * (1.0 / (4.0 * BLOCK * BLOCK))
    amplitude = jnp.exp(-radius)
    angle = focus * radius
    quarter = jnp.floor(angle * (2.0 / math.pi) + 0.5)
    angle = angle - quarter * 1.5703125
    angle = angle - quarter * 4.837512969970703e-4
    angle = angle - quarter * 7.549789954891882e-8
    cosine, sine = turn_by(angle, quarter.astype(jnp.int32))
    return amplitude * cosine, amplitude * sine


def table_kernel(place_ref, rowf_ref, colf_ref):
    first_row, first_column = place_ref[0], place_ref[1]
    u = lax.broadcasted_iota(jnp.int32, (BLOCK, XR), 0) - SPEC // 2
    x = lax.broadcasted_iota(jnp.int32, (BLOCK, XR), 1) + first_row
    y = lax.broadcasted_iota(jnp.int32, (ROWS, BLOCK), 0) + first_column
    lane = lax.broadcasted_iota(jnp.int32, (ROWS, BLOCK), 1)
    v = (lane & 31) * 4 + (lane >> 5) - SPEC // 2

    def body(n, carry):
        cosine, sine = phases((u + n * BLOCK) * x)
        cosine, sine, minus = cosine.astype(BF16), sine.astype(BF16), (-sine).astype(BF16)
        rowf_ref[n, :BLOCK, :XR] = cosine
        rowf_ref[n, :BLOCK, XR:] = sine
        rowf_ref[n, BLOCK:, :XR] = minus
        rowf_ref[n, BLOCK:, XR:] = cosine
        both = jnp.concatenate(phases((v + n * BLOCK) * y), axis=0)
        colf_ref[n, 0] = both.astype(BF16)
        for d in (1, 2, 3):
            colf_ref[n, d] = pltpu.roll(both, 32 * d, 1).astype(BF16)
        return carry

    lax.fori_loop(0, NB, body, 0)
    colf_ref[NB] = jnp.zeros((4, 2 * ROWS, BLOCK), BF16)


def round_bf16(value):
    return value.astype(BF16).astype(F32)


def pack_kernel(core_ref, centers_ref, counts_ref, weights_ref, blocks_ref, spectrum_ref, out_ref):
    start = pl.multiple_of(512 * core_ref[0], 512)
    half = spectrum_ref[:, :, pl.ds(start, 512)].astype(F32).reshape(16, 512).astype(BF16)
    rows = lax.broadcasted_iota(jnp.int32, (BLOCK, BLOCK), 0)
    lanes = lax.broadcasted_iota(jnp.int32, (BLOCK, BLOCK), 1)
    select = (rows == (lanes & 31) * 4 + (lanes >> 5)).astype(F32).astype(BF16)
    parts = [
        jnp.dot(half[:, 128 * j:128 * j + 128], select, preferred_element_type=F32).astype(BF16)
        for j in range(4)
    ]
    numbers = [centers_ref[0, 0], centers_ref[0, 1], counts_ref[0, 0].astype(F32), weights_ref[0, 0]]
    numbers += [blocks_ref[0, k].astype(F32) for k in range(SLOTS)]
    lane = lax.broadcasted_iota(jnp.int32, (16, 128), 1)
    info = jnp.zeros((16, 128), F32)
    for n, value in enumerate(numbers):
        info = jnp.where(lane & 15 == n, value, info)
    high = round_bf16(info)
    mid = round_bf16(info - high)
    low = info - high - mid
    info = jnp.where(lane < 16, high, jnp.where(lane < 32, mid, low)).astype(BF16)
    for n in range(8):
        for j in range(4):
            out_ref[n, j] = parts[j]
        out_ref[n, 4] = info


def spread_kernel(column_ref, out_ref):
    row = lax.broadcasted_iota(jnp.int32, (16, 128), 0)
    info = jnp.zeros((16, 128), F32)
    for n in range(8):
        info = jnp.where(row == n, column_ref[n, 4].astype(F32)[0:1], info)
    info = info.astype(BF16)
    for m in range(4):
        for n in range(8):
            out_ref[m, 4 * n:4 * n + 4] = column_ref[n, :4]
        out_ref[m, 32] = info


def turned_block(rows_ref, at, carrier):
    parts = [
        rows_ref[jnp.where(carrier == 1, 4 * (n % 4) + n // 4, n), at].astype(F32) for n in range(16)
    ]
    stack = jnp.concatenate([p[:8] for p in parts] + [p[8:] for p in parts], axis=0)
    return jnp.transpose(stack.astype(BF16))


def turn_kernel(core_ref, rows_ref, out_ref):
    for n in range(8):
        out_ref[n] = turned_block(rows_ref, n, core_ref[0])


def image_kernel(
    info_ref, whole_ref, focus_ref, core_ref, own_ref, other_ref, rows_ref, columns_ref,
    keep_ref, send_ref, raw, turned, rowf_ref, colf_ref, pieces, power, even, odd, numbers, p_re, p_im, q_re, q_im, listing, sems,
):
    def count_of(s):
        return whole_ref[16 * s + 2]

    def block_of(e):
        return whole_ref[((e >> 3) << 4) + 4 + (e & 7)]

    copies = [
        pltpu.make_async_copy(ref, place, sems.at[n])
        for n, (ref, place) in enumerate(
            (
                (other_ref, raw),
                (own_ref, turned.at[pl.ds(0, 32)]),
                (rows_ref, rowf_ref),
                (columns_ref, colf_ref),
            )
        )
    ]
    for copy in copies[:3]:
        copy.start()

    def live(s, total):
        for k in range(SLOTS):
            listing[total + k] = s * SLOTS + k
        return total + count_of(s)

    total = lax.fori_loop(0, LOCAL, live, 0)
    for n in range(GROUP):
        listing[total + n] = ENTRIES
    groups = (total + GROUP - 1) >> 4
    lane = lax.broadcasted_iota(jnp.int32, (SLOTS, BLOCK), 1)
    by_residue = ((lane & 31) * 4 + (lane >> 5)).astype(F32)
    lane = lane.astype(F32)
    for s in range(LOCAL):
        rows = slice(SLOTS * s, SLOTS * s + SLOTS)
        for k in range(SLOTS):
            numbers[SLOTS * s + k:SLOTS * s + k + 1, :] = jnp.full((1, BLOCK), info_ref[16 * s + 4 + k])
        number = numbers[rows, :]
        i = jnp.floor(number * (1.0 / NB))
        j = number - i * NB
        p_re[rows, :], p_im[rows, :] = pupil_factor(i * BLOCK + lane - info_ref[16 * s], focus_ref[0])
        q_re[rows, :], q_im[rows, :] = pupil_factor(j * BLOCK + by_residue - info_ref[16 * s + 1], focus_ref[0])

    pieces[...] = jnp.zeros_like(pieces)
    power[...] = jnp.zeros_like(power)
    copies[0].wait()
    copies[3].start()

    def turn(n, carry):
        for m in range(8):
            turned[32 + 8 * n + m] = turned_block(raw, 8 * n + m, 1 - core_ref[0])
        return carry

    lax.fori_loop(0, 4, turn, 0)
    copies[1].wait()
    copies[2].wait()

    def entries(g, carry):
        places = [listing[g * GROUP + n] for n in range(GROUP)]
        sources = [jnp.minimum(e, ENTRIES - 1) for e in places]
        q_all = jnp.transpose(
            jnp.concatenate([part[pl.ds(e, 1), :] for part in (q_re, q_im) for e in sources], axis=0)
        )
        for n in range(GROUP):
            number = block_of(sources[n])
            i, j = number >> 3, number & 7
            block = turned[(((j >> 2) ^ core_ref[0]) << 5) + (i << 2) + (j & 3)].astype(F32)
            re, im = block[:, :128], block[:, 128:]
            pr, pi = p_re[pl.ds(sources[n], 1), :], p_im[pl.ds(sources[n], 1), :]
            qr, qi = q_all[:, n:n + 1], q_all[:, GROUP + n:GROUP + n + 1]
            pupil_re = qr * pr - qi * pi
            pupil_im = qr * pi + qi * pr
            masked_re = (re * pupil_re - im * pupil_im).astype(BF16)
            masked_im = (re * pupil_im + im * pupil_re).astype(BF16)
            masked = jnp.concatenate([masked_re, masked_im], axis=1)
            piece = jnp.dot(masked, rowf_ref[i], preferred_element_type=F32).astype(BF16)
            place = pl.ds(pl.multiple_of(32 * (places[n] & 7), 32), 32)
            for r in range(4):
                pieces[places[n] >> 3, r, place, :] = piece[32 * r:32 * r + 32]
        return carry

    lax.fori_loop(0, groups, entries, 0)
    copies[3].wait()

    lane_group = lax.broadcasted_iota(jnp.int32, (2 * ROWS, 128), 1) // 32

    def transform(s, buffer):
        columns = [
            jnp.where(k < count_of(s), whole_ref[16 * s + 4 + k] & 7, NB) for k in range(SLOTS)
        ]
        for r in range(4):
            halves = []
            for h in range(2):
                table = None
                for m in range(4):
                    term = colf_ref[columns[4 * h + m], (m - r) % 4]
                    table = term if table is None else jnp.where(lane_group == m, term, table)
                halves.append(table)
            table = jnp.concatenate(halves, axis=1)
            buffer[r] = jnp.dot(table, pieces[s, r], preferred_element_type=F32)

    def gather_power(s, buffer):
        weight = info_ref[16 * s + 3]
        for c in range(ROWS // 8):
            low = slice(8 * c, 8 * c + 8)
            high = slice(ROWS + 8 * c, ROWS + 8 * c + 8)
            direct, mirror = [], []
            for r in range(4):
                a_cos, b_cos = buffer[r, low, :128], buffer[r, low, 128:]
                a_sin, b_sin = buffer[r, high, :128], buffer[r, high, 128:]
                direct.append((a_cos - b_sin, a_sin + b_cos))
                mirror.append((a_cos + b_sin, b_cos - a_sin))
            for base, parts in ((0, direct), (4, mirror)):
                (r0, i0), (r1, i1), (r2, i2), (r3, i3) = parts
                gr, gi, dr, di = r0 + r2, i0 + i2, r0 - r2, i0 - i2
                hr, hi, er, ei = r1 + r3, i1 + i3, r1 - r3, i1 - i3
                images = ((gr + hr, gi + hi), (dr - ei, di + er), (gr - hr, gi - hi), (dr + ei, di - er))
                for m, (fr, fi) in enumerate(images):
                    power[base + m, low] += weight * (fr * fr + fi * fi)

    transform(0, even)
    def two(i, carry):
        gather_power(2 * i, even)
        transform(2 * i + 1, odd)
        gather_power(2 * i + 1, odd)
        transform(jnp.minimum(2 * i + 2, LOCAL - 1), even)
        return carry
    lax.fori_loop(0, LOCAL // 2, two, 0)
    mine = pl.multiple_of(PART * core_ref[0], PART)
    theirs = pl.multiple_of(PART * (1 - core_ref[0]), PART)
    for image in range(8):
        keep_ref[image] = power[image, pl.ds(mine, PART_ROWS), :]
        send_ref[image] = power[image, pl.ds(theirs, PART_ROWS), :]


def slope_kernel(dose_ref, keep_ref, other_ref, out_ref):
    dose = dose_ref[0]
    for e in range(8):
        image = e // 2 if e % 2 == 0 else 4 + (e // 2 + 1) % 4
        low = 1 + e % 2
        level = dose * (keep_ref[image] + other_ref[image]) / SOURCES + BACKGROUND
        slope = jnp.abs(level[low + 1:low + 1 + PART] - level[low - 1:low - 1 + PART]) / (
            2.0 * level[low:low + PART]
        )
        out_ref[e] = jnp.exp(slope * (-1.0 / TAU))


def on_device(spectrum, centers, blocks, counts, weights, defocus, dose_scale):
    core = lax.axis_index("cond")
    source = lax.axis_index("source")
    z, y = source // 4, source % 4
    swap = [(0, 1), (1, 0)]
    vmem = pl.BlockSpec(memory_space=pltpu.VMEM)
    smem = pl.BlockSpec(memory_space=pltpu.SMEM)
    hbm = pl.BlockSpec(memory_space=pl.ANY)
    packed = pl.pallas_call(
        pack_kernel,
        out_shape=jax.ShapeDtypeStruct((8, 5, 16, 128), BF16),
        in_specs=[smem] * 5 + [vmem],
        out_specs=vmem,
        compiler_params=pltpu.CompilerParams(vmem_limit_bytes=56 * MIB),
    )(core.reshape(1), centers, counts.reshape(1, 1), weights.reshape(1, 1), blocks, spectrum)
    column = lax.all_to_all(packed, "source", 0, 0, axis_index_groups=Z_GROUPS)
    copies = pl.pallas_call(
        spread_kernel,
        out_shape=jax.ShapeDtypeStruct((4, 33, 16, 128), BF16),
        in_specs=[vmem],
        out_specs=vmem,
        compiler_params=pltpu.CompilerParams(vmem_limit_bytes=4 * MIB),
    )(column)
    every = ("source", "row", "cond")
    line = lax.all_to_all(copies, every, 0, 0, axis_index_groups=X_LINES[0] + Y_LINES[1])
    defocus, dose_scale, line = lax.optimization_barrier((defocus, dose_scale, line))

    local = jnp.concatenate([defocus, dose_scale])
    remote = lax.ppermute(local, "cond", swap)
    cond = z % 4
    chosen = jnp.where(cond // 2 == core, local, remote)
    focus = jnp.where(cond % 2 == 0, chosen[0], chosen[1])
    dose = jnp.where(cond % 2 == 0, chosen[2], chosen[3])
    quarter = jnp.where(z % 2 == 0, y, 3 - y)
    window = 2 * quarter + z // 4
    place = jnp.stack([lax.axis_index("row") * XR, window * W - 1])
    place, line = lax.optimization_barrier((place, line))
    rowf, colf = pl.pallas_call(
        table_kernel,
        out_shape=[
            jax.ShapeDtypeStruct((NB, 2 * BLOCK, 2 * XR), BF16),
            jax.ShapeDtypeStruct((NB + 1, 4, 2 * ROWS, BLOCK), BF16),
        ],
        in_specs=[smem],
        out_specs=[vmem, vmem],
        compiler_params=pltpu.CompilerParams(vmem_limit_bytes=56 * MIB),
    )(place)

    copies = jnp.broadcast_to(line[None], (4, 4, 33, 16, 128))
    rows = lax.all_to_all(copies, every, 0, 0, axis_index_groups=Y_LINES[0] + X_LINES[1])
    rows = rows.reshape(16, 33, 16, 128)
    rows, rowf, colf, dose, focus = lax.optimization_barrier((rows, rowf, colf, dose, focus))
    own = pl.pallas_call(
        turn_kernel,
        grid=(4,),
        out_shape=jax.ShapeDtypeStruct((32, 128, 256), BF16),
        in_specs=[smem, pl.BlockSpec((16, 8, 16, 128), lambda i: (0, i, 0, 0))],
        out_specs=pl.BlockSpec((8, 128, 256), lambda i: (i, 0, 0)),
        compiler_params=pltpu.CompilerParams(vmem_limit_bytes=8 * MIB),
    )(core.reshape(1), rows)
    other = lax.ppermute(rows, "cond", swap)

    tiles = rows[:5, 32, :8, :48]
    info = jnp.stack([jnp.where(core == 0, tiles[0], tiles[2]), jnp.where(core == 0, tiles[4], tiles[3])]).astype(F32)
    info = (info[:, :, :16] + info[:, :, 16:32] + info[:, :, 32:]).reshape(-1)
    keep, send = pl.pallas_call(
        image_kernel,
        out_shape=[jax.ShapeDtypeStruct((8, PART_ROWS, XR), F32)] * 2,
        in_specs=[smem] * 4 + [hbm] * 4,
        out_specs=[vmem] * 2,
        scratch_shapes=[
            pltpu.VMEM((16, 33, 16, 128), BF16),
            pltpu.VMEM((64, 128, 256), BF16),
            pltpu.VMEM((NB, 2 * BLOCK, 2 * XR), BF16),
            pltpu.VMEM((NB + 1, 4, 2 * ROWS, BLOCK), BF16),
            pltpu.VMEM((LOCAL + 1, 4, 256, 256), BF16),
            pltpu.VMEM((8, ROWS, XR), F32),
            pltpu.VMEM((4, 2 * ROWS, 256), F32),
            pltpu.VMEM((4, 2 * ROWS, 256), F32),
        ] + [pltpu.VMEM((ENTRIES, BLOCK), F32)] * 5 + [
            pltpu.SMEM((ENTRIES + GROUP,), jnp.int32),
            pltpu.SemaphoreType.DMA((4,)),
        ],
        compiler_params=pltpu.CompilerParams(vmem_limit_bytes=56 * MIB),
    )(info, info.astype(jnp.int32), focus.reshape(1), core.reshape(1), own, other, rowf, colf)
    received = lax.ppermute(send, "cond", swap)
    terms = pl.pallas_call(
        slope_kernel,
        out_shape=jax.ShapeDtypeStruct((8, PART, XR), F32),
        in_specs=[smem, vmem, vmem],
        out_specs=vmem,
        compiler_params=pltpu.CompilerParams(vmem_limit_bytes=4 * MIB),
    )(dose.reshape(1), keep, received)
    terms = lax.all_to_all(terms, "source", 0, 0, axis_index_groups=TILE_GROUPS)
    soft = -TAU * jnp.log(jnp.sum(terms.reshape(2, CONDS, PART, XR), axis=1) / CONDS)
    theirs = lax.ppermute(soft, "cond", swap)
    first, second = jnp.where(core == 0, soft, theirs), jnp.where(core == 0, theirs, soft)
    soft = jnp.stack([first, second], axis=1).reshape(2 * W, XR)
    soft = jnp.where(z % 2 == 0, soft, soft[::-1])
    return soft.T


def solution(mesh):
    in_specs = (
        P(None, ("source", "row"), None),
        P("source", None),
        P("source", None),
        P("source"),
        P("source"),
        P("cond"),
        P("cond"),
    )
    out_specs = P("row", "source")
    return jax.shard_map(
        on_device, mesh=mesh, in_specs=in_specs, out_specs=out_specs, check_vma=False
    )
```

```python
import functools
import math

import jax
import jax.numpy as jnp
from jax import lax
from jax.experimental import pallas as pl
from jax.experimental.pallas import tpu as pltpu
from jax.sharding import PartitionSpec as P

N = 4096
BLOCK = 128
NB = 8
XR = 128
SPEC = 1024
SOURCES = 32
SLOTS = 8
CONDS = 4
W = 64
ROWS = 72
PART = 32
PART_ROWS = 40
GROUP = 16
LOCAL = SOURCES // 2
ENTRIES = LOCAL * SLOTS

TAU = 0.5
BACKGROUND = 0.05

MIB = 1024 * 1024
F32 = jnp.float32
BF16 = jnp.bfloat16

Z_GROUPS = [[z * 4 + y for z in range(8)] for y in range(4)]
X_LINES = [[[((z * 4 + y) * 4 + x) * 2 + c for x in range(4)] for z in range(8) for y in range(4)] for c in range(2)]
Y_LINES = [[[((z * 4 + y) * 4 + x) * 2 + c for y in range(4)] for z in range(8) for x in range(4)] for c in range(2)]
TILE_GROUPS = [[8 * k + t for k in range(4) for t in (q, 7 - q)] for q in range(4)]


def turn_by(angle, quarter):
    square = angle * angle
    sine = 1.0 + square * (-1.0 / 6.0 + square * (1.0 / 120.0 + square * (-1.0 / 5040.0 + square * (1.0 / 362880.0))))
    sine = angle * sine
    cosine = 1.0 + square * (-0.5 + square * (1.0 / 24.0 + square * (-1.0 / 720.0 + square * (1.0 / 40320.0))))
    odd = (quarter & 1) == 1
    first, second = jnp.where(odd, sine, cosine), jnp.where(odd, cosine, sine)
    cosine = jnp.where(((quarter + 1) & 2) == 2, -first, first)
    sine = jnp.where((quarter & 2) == 2, -second, second)
    return cosine, sine


def phases(product):
    turn = product & (N - 1)
    quarter = (turn + N // 8) >> 10
    return turn_by((turn - (quarter << 10)).astype(F32) * (2.0 * math.pi / N), quarter)


def pupil_factor(gap, focus):
    radius = gap * gap * (1.0 / (4.0 * BLOCK * BLOCK))
    amplitude = jnp.exp(-radius)
    angle = focus * radius
    quarter = jnp.floor(angle * (2.0 / math.pi) + 0.5)
    angle = angle - quarter * 1.5703125
    angle = angle - quarter * 4.837512969970703e-4
    angle = angle - quarter * 7.549789954891882e-8
    cosine, sine = turn_by(angle, quarter.astype(jnp.int32))
    return amplitude * cosine, amplitude * sine


def table_kernel(place_ref, rowf_ref, colf_ref):
    first_row, first_column = place_ref[0], place_ref[1]
    u = lax.broadcasted_iota(jnp.int32, (BLOCK, XR), 0) - SPEC // 2
    x = lax.broadcasted_iota(jnp.int32, (BLOCK, XR), 1) + first_row
    y = lax.broadcasted_iota(jnp.int32, (ROWS, BLOCK), 0) + first_column
    lane = lax.broadcasted_iota(jnp.int32, (ROWS, BLOCK), 1)
    v = (lane & 31) * 4 + (lane >> 5) - SPEC // 2

    def body(n, carry):
        cosine, sine = phases((u + n * BLOCK) * x)
        cosine, sine, minus = cosine.astype(BF16), sine.astype(BF16), (-sine).astype(BF16)
        rowf_ref[n, :BLOCK, :XR] = cosine
        rowf_ref[n, :BLOCK, XR:] = sine
        rowf_ref[n, BLOCK:, :XR] = minus
        rowf_ref[n, BLOCK:, XR:] = cosine
        both = jnp.concatenate(phases((v + n * BLOCK) * y), axis=0)
        colf_ref[n, 0] = both.astype(BF16)
        for d in (1, 2, 3):
            colf_ref[n, d] = pltpu.roll(both, 32 * d, 1).astype(BF16)
        return carry

    lax.fori_loop(0, NB, body, 0)
    colf_ref[NB] = jnp.zeros((4, 2 * ROWS, BLOCK), BF16)


def round_bf16(value):
    return value.astype(BF16).astype(F32)


def pack_kernel(core_ref, centers_ref, counts_ref, weights_ref, blocks_ref, spectrum_ref, out_ref):
    start = pl.multiple_of(512 * core_ref[0], 512)
    half = spectrum_ref[:, :, pl.ds(start, 512)].astype(F32).reshape(16, 512).astype(BF16)
    rows = lax.broadcasted_iota(jnp.int32, (BLOCK, BLOCK), 0)
    lanes = lax.broadcasted_iota(jnp.int32, (BLOCK, BLOCK), 1)
    select = (rows == (lanes & 31) * 4 + (lanes >> 5)).astype(F32).astype(BF16)
    parts = [
        jnp.dot(half[:, 128 * j:128 * j + 128], select, preferred_element_type=F32).astype(BF16)
        for j in range(4)
    ]
    numbers = [centers_ref[0, 0], centers_ref[0, 1], counts_ref[0, 0].astype(F32), weights_ref[0, 0]]
    numbers += [blocks_ref[0, k].astype(F32) for k in range(SLOTS)]
    lane = lax.broadcasted_iota(jnp.int32, (16, 128), 1)
    info = jnp.zeros((16, 128), F32)
    for n, value in enumerate(numbers):
        info = jnp.where(lane & 15 == n, value, info)
    high = round_bf16(info)
    mid = round_bf16(info - high)
    low = info - high - mid
    info = jnp.where(lane < 16, high, jnp.where(lane < 32, mid, low)).astype(BF16)
    for n in range(8):
        for j in range(4):
            out_ref[n, j] = parts[j]
        out_ref[n, 4] = info


def spread_kernel(column_ref, out_ref):
    row = lax.broadcasted_iota(jnp.int32, (16, 128), 0)
    info = jnp.zeros((16, 128), F32)
    for n in range(8):
        info = jnp.where(row == n, column_ref[n, 4].astype(F32)[0:1], info)
    info = info.astype(BF16)
    for m in range(4):
        for n in range(8):
            out_ref[m, 4 * n:4 * n + 4] = column_ref[n, :4]
        out_ref[m, 32] = info


def turned_block(rows_ref, at, carrier):
    parts = [
        rows_ref[jnp.where(carrier == 1, 4 * (n % 4) + n // 4, n), at].astype(F32) for n in range(16)
    ]
    stack = jnp.concatenate([p[:8] for p in parts] + [p[8:] for p in parts], axis=0)
    return jnp.transpose(stack.astype(BF16))


def turn_kernel(core_ref, rows_ref, out_ref):
    for n in range(8):
        out_ref[n] = turned_block(rows_ref, n, core_ref[0])


def image_kernel(
    info_ref, whole_ref, focus_ref, core_ref, own_ref, other_ref, rows_ref, columns_ref,
    keep_ref, send_ref, raw, turned, rowf_ref, colf_ref, pieces, power, even, odd, numbers, center_u, center_v, p_re, p_im, q_re, q_im, listing, sems,
):
    def count_of(s):
        return whole_ref[16 * s + 2]

    def block_of(e):
        return whole_ref[((e >> 3) << 4) + 4 + (e & 7)]

    copies = [
        pltpu.make_async_copy(ref, place, sems.at[n])
        for n, (ref, place) in enumerate(
            (
                (other_ref, raw),
                (own_ref, turned.at[pl.ds(0, 32)]),
                (rows_ref, rowf_ref),
                (columns_ref, colf_ref),
            )
        )
    ]
    for copy in copies[:3]:
        copy.start()

    def live(s, total):
        rows = pl.ds(total, SLOTS)
        center_u[rows, :] = jnp.full((SLOTS, BLOCK), info_ref[16 * s])
        center_v[rows, :] = jnp.full((SLOTS, BLOCK), info_ref[16 * s + 1])
        for k in range(SLOTS):
            listing[total + k] = s * SLOTS + k
            numbers[pl.ds(total + k, 1), :] = jnp.full((1, BLOCK), info_ref[16 * s + 4 + k])
        return total + count_of(s)

    total = lax.fori_loop(0, LOCAL, live, 0)
    for n in range(GROUP):
        listing[total + n] = ENTRIES
    groups = (total + GROUP - 1) >> 4
    lane = lax.broadcasted_iota(jnp.int32, (GROUP, BLOCK), 1)
    by_residue = ((lane & 31) * 4 + (lane >> 5)).astype(F32)
    lane = lane.astype(F32)

    def factors(g, carry):
        rows = pl.ds(pl.multiple_of(GROUP * g, GROUP), GROUP)
        number = numbers[rows, :]
        i = jnp.floor(number * (1.0 / NB))
        j = number - i * NB
        p_re[rows, :], p_im[rows, :] = pupil_factor(i * BLOCK + lane - center_u[rows, :], focus_ref[0])
        q_re[rows, :], q_im[rows, :] = pupil_factor(j * BLOCK + by_residue - center_v[rows, :], focus_ref[0])
        return carry

    lax.fori_loop(0, groups, factors, 0)

    pieces[...] = jnp.zeros_like(pieces)
    power[...] = jnp.zeros_like(power)
    copies[0].wait()
    copies[3].start()

    def turn(n, carry):
        for m in range(8):
            turned[32 + 8 * n + m] = turned_block(raw, 8 * n + m, 1 - core_ref[0])
        return carry

    lax.fori_loop(0, 4, turn, 0)
    copies[1].wait()
    copies[2].wait()

    def entries(g, carry):
        places = [listing[g * GROUP + n] for n in range(GROUP)]
        sources = [jnp.minimum(e, ENTRIES - 1) for e in places]
        rows = pl.ds(pl.multiple_of(GROUP * g, GROUP), GROUP)
        pr_all, pi_all = p_re[rows, :], p_im[rows, :]
        q_all = jnp.transpose(jnp.concatenate([q_re[rows, :], q_im[rows, :]], axis=0))
        for n in range(GROUP):
            number = block_of(sources[n])
            i, j = number >> 3, number & 7
            block = turned[(((j >> 2) ^ core_ref[0]) << 5) + (i << 2) + (j & 3)].astype(F32)
            re, im = block[:, :128], block[:, 128:]
            pr, pi = pr_all[n:n + 1], pi_all[n:n + 1]
            qr, qi = q_all[:, n:n + 1], q_all[:, GROUP + n:GROUP + n + 1]
            pupil_re = qr * pr - qi * pi
            pupil_im = qr * pi + qi * pr
            masked_re = (re * pupil_re - im * pupil_im).astype(BF16)
            masked_im = (re * pupil_im + im * pupil_re).astype(BF16)
            masked = jnp.concatenate([masked_re, masked_im], axis=1)
            piece = jnp.dot(masked, rowf_ref[i], preferred_element_type=F32).astype(BF16)
            place = pl.ds(pl.multiple_of(32 * (places[n] & 7), 32), 32)
            for r in range(4):
                pieces[places[n] >> 3, r, place, :] = piece[32 * r:32 * r + 32]
        return carry

    lax.fori_loop(0, groups, entries, 0)
    copies[3].wait()

    lane_group = lax.broadcasted_iota(jnp.int32, (2 * ROWS, 128), 1) // 32

    def transform(s, buffer):
        columns = [
            jnp.where(k < count_of(s), whole_ref[16 * s + 4 + k] & 7, NB) for k in range(SLOTS)
        ]
        for r in range(4):
            halves = []
            for h in range(2):
                table = None
                for m in range(4):
                    term = colf_ref[columns[4 * h + m], (m - r) % 4]
                    table = term if table is None else jnp.where(lane_group == m, term, table)
                halves.append(table)
            table = jnp.concatenate(halves, axis=1)
            buffer[r] = jnp.dot(table, pieces[s, r], preferred_element_type=F32)

    def gather_power(s, buffer):
        weight = info_ref[16 * s + 3]
        for c in range(ROWS // 8):
            low = slice(8 * c, 8 * c + 8)
            high = slice(ROWS + 8 * c, ROWS + 8 * c + 8)
            direct, mirror = [], []
            for r in range(4):
                a_cos, b_cos = buffer[r, low, :128], buffer[r, low, 128:]
                a_sin, b_sin = buffer[r, high, :128], buffer[r, high, 128:]
                direct.append((a_cos - b_sin, a_sin + b_cos))
                mirror.append((a_cos + b_sin, b_cos - a_sin))
            for base, parts in ((0, direct), (4, mirror)):
                (r0, i0), (r1, i1), (r2, i2), (r3, i3) = parts
                gr, gi, dr, di = r0 + r2, i0 + i2, r0 - r2, i0 - i2
                hr, hi, er, ei = r1 + r3, i1 + i3, r1 - r3, i1 - i3
                images = ((gr + hr, gi + hi), (dr - ei, di + er), (gr - hr, gi - hi), (dr + ei, di - er))
                for m, (fr, fi) in enumerate(images):
                    power[base + m, low] += weight * (fr * fr + fi * fi)

    transform(0, even)
    def two(i, carry):
        gather_power(2 * i, even)
        transform(2 * i + 1, odd)
        gather_power(2 * i + 1, odd)
        transform(jnp.minimum(2 * i + 2, LOCAL - 1), even)
        return carry
    lax.fori_loop(0, LOCAL // 2, two, 0)
    mine = pl.multiple_of(PART * core_ref[0], PART)
    theirs = pl.multiple_of(PART * (1 - core_ref[0]), PART)
    for image in range(8):
        keep_ref[image] = power[image, pl.ds(mine, PART_ROWS), :]
        send_ref[image] = power[image, pl.ds(theirs, PART_ROWS), :]


def slope_kernel(dose_ref, keep_ref, other_ref, out_ref):
    dose = dose_ref[0]
    for e in range(8):
        image = e // 2 if e % 2 == 0 else 4 + (e // 2 + 1) % 4
        low = 1 + e % 2
        level = dose * (keep_ref[image] + other_ref[image]) / SOURCES + BACKGROUND
        slope = jnp.abs(level[low + 1:low + 1 + PART] - level[low - 1:low - 1 + PART]) / (
            2.0 * level[low:low + PART]
        )
        out_ref[e] = jnp.exp(slope * (-1.0 / TAU))


def on_device(spectrum, centers, blocks, counts, weights, defocus, dose_scale):
    core = lax.axis_index("cond")
    source = lax.axis_index("source")
    z, y = source // 4, source % 4
    swap = [(0, 1), (1, 0)]
    vmem = pl.BlockSpec(memory_space=pltpu.VMEM)
    smem = pl.BlockSpec(memory_space=pltpu.SMEM)
    hbm = pl.BlockSpec(memory_space=pl.ANY)
    packed = pl.pallas_call(
        pack_kernel,
        out_shape=jax.ShapeDtypeStruct((8, 5, 16, 128), BF16),
        in_specs=[smem] * 5 + [vmem],
        out_specs=vmem,
        compiler_params=pltpu.CompilerParams(vmem_limit_bytes=56 * MIB),
    )(core.reshape(1), centers, counts.reshape(1, 1), weights.reshape(1, 1), blocks, spectrum)
    column = lax.all_to_all(packed, "source", 0, 0, axis_index_groups=Z_GROUPS)
    copies = pl.pallas_call(
        spread_kernel,
        out_shape=jax.ShapeDtypeStruct((4, 33, 16, 128), BF16),
        in_specs=[vmem],
        out_specs=vmem,
        compiler_params=pltpu.CompilerParams(vmem_limit_bytes=4 * MIB),
    )(column)
    every = ("source", "row", "cond")
    line = lax.all_to_all(copies, every, 0, 0, axis_index_groups=X_LINES[0] + Y_LINES[1])
    defocus, dose_scale, line = lax.optimization_barrier((defocus, dose_scale, line))

    local = jnp.concatenate([defocus, dose_scale])
    remote = lax.ppermute(local, "cond", swap)
    cond = z % 4
    chosen = jnp.where(cond // 2 == core, local, remote)
    focus = jnp.where(cond % 2 == 0, chosen[0], chosen[1])
    dose = jnp.where(cond % 2 == 0, chosen[2], chosen[3])
    quarter = jnp.where(z % 2 == 0, y, 3 - y)
    window = 2 * quarter + z // 4
    place = jnp.stack([lax.axis_index("row") * XR, window * W - 1])
    place, line = lax.optimization_barrier((place, line))
    rowf, colf = pl.pallas_call(
        table_kernel,
        out_shape=[
            jax.ShapeDtypeStruct((NB, 2 * BLOCK, 2 * XR), BF16),
            jax.ShapeDtypeStruct((NB + 1, 4, 2 * ROWS, BLOCK), BF16),
        ],
        in_specs=[smem],
        out_specs=[vmem, vmem],
        compiler_params=pltpu.CompilerParams(vmem_limit_bytes=56 * MIB),
    )(place)

    copies = jnp.broadcast_to(line[None], (4, 4, 33, 16, 128))
    rows = lax.all_to_all(copies, every, 0, 0, axis_index_groups=Y_LINES[0] + X_LINES[1])
    rows = rows.reshape(16, 33, 16, 128)
    rows, rowf, colf, dose, focus = lax.optimization_barrier((rows, rowf, colf, dose, focus))
    own = pl.pallas_call(
        turn_kernel,
        grid=(4,),
        out_shape=jax.ShapeDtypeStruct((32, 128, 256), BF16),
        in_specs=[smem, pl.BlockSpec((16, 8, 16, 128), lambda i: (0, i, 0, 0))],
        out_specs=pl.BlockSpec((8, 128, 256), lambda i: (i, 0, 0)),
        compiler_params=pltpu.CompilerParams(vmem_limit_bytes=8 * MIB),
    )(core.reshape(1), rows)
    other = lax.ppermute(rows, "cond", swap)

    tiles = rows[:5, 32, :8, :48]
    info = jnp.stack([jnp.where(core == 0, tiles[0], tiles[2]), jnp.where(core == 0, tiles[4], tiles[3])]).astype(F32)
    info = (info[:, :, :16] + info[:, :, 16:32] + info[:, :, 32:]).reshape(-1)
    keep, send = pl.pallas_call(
        image_kernel,
        out_shape=[jax.ShapeDtypeStruct((8, PART_ROWS, XR), F32)] * 2,
        in_specs=[smem] * 4 + [hbm] * 4,
        out_specs=[vmem] * 2,
        scratch_shapes=[
            pltpu.VMEM((16, 33, 16, 128), BF16),
            pltpu.VMEM((64, 128, 256), BF16),
            pltpu.VMEM((NB, 2 * BLOCK, 2 * XR), BF16),
            pltpu.VMEM((NB + 1, 4, 2 * ROWS, BLOCK), BF16),
            pltpu.VMEM((LOCAL + 1, 4, 256, 256), BF16),
            pltpu.VMEM((8, ROWS, XR), F32),
            pltpu.VMEM((4, 2 * ROWS, 256), F32),
            pltpu.VMEM((4, 2 * ROWS, 256), F32),
        ] + [pltpu.VMEM((ENTRIES + SLOTS, BLOCK), F32)] * 7 + [
            pltpu.SMEM((ENTRIES + GROUP,), jnp.int32),
            pltpu.SemaphoreType.DMA((4,)),
        ],
        compiler_params=pltpu.CompilerParams(vmem_limit_bytes=52 * MIB),
    )(info, info.astype(jnp.int32), focus.reshape(1), core.reshape(1), own, other, rowf, colf)
    received = lax.ppermute(send, "cond", swap)
    terms = pl.pallas_call(
        slope_kernel,
        out_shape=jax.ShapeDtypeStruct((8, PART, XR), F32),
        in_specs=[smem, vmem, vmem],
        out_specs=vmem,
        compiler_params=pltpu.CompilerParams(vmem_limit_bytes=4 * MIB),
    )(dose.reshape(1), keep, received)
    terms = lax.all_to_all(terms, "source", 0, 0, axis_index_groups=TILE_GROUPS)
    soft = -TAU * jnp.log(jnp.sum(terms.reshape(2, CONDS, PART, XR), axis=1) / CONDS)
    theirs = lax.ppermute(soft, "cond", swap)
    first, second = jnp.where(core == 0, soft, theirs), jnp.where(core == 0, theirs, soft)
    soft = jnp.stack([first, second], axis=1).reshape(2 * W, XR)
    soft = jnp.where(z % 2 == 0, soft, soft[::-1])
    return soft.T


def solution(mesh):
    in_specs = (
        P(None, ("source", "row"), None),
        P("source", None),
        P("source", None),
        P("source"),
        P("source"),
        P("cond"),
        P("cond"),
    )
    out_specs = P("row", "source")
    return jax.shard_map(
        on_device, mesh=mesh, in_specs=in_specs, out_specs=out_specs, check_vma=False
    )
```

```python
import functools
import math

import jax
import jax.numpy as jnp
from jax import lax
from jax.experimental import pallas as pl
from jax.experimental.pallas import tpu as pltpu
from jax.sharding import PartitionSpec as P

N = 4096
BLOCK = 128
NB = 8
XR = 128
SPEC = 1024
SOURCES = 32
SLOTS = 8
CONDS = 4
W = 64
ROWS = 72
PART = 32
PART_ROWS = 40
GROUP = 16
LOCAL = SOURCES // 2
ENTRIES = LOCAL * SLOTS

TAU = 0.5
BACKGROUND = 0.05

MIB = 1024 * 1024
F32 = jnp.float32
BF16 = jnp.bfloat16

Z_GROUPS = [[z * 4 + y for z in range(8)] for y in range(4)]
X_LINES = [[[((z * 4 + y) * 4 + x) * 2 + c for x in range(4)] for z in range(8) for y in range(4)] for c in range(2)]
Y_LINES = [[[((z * 4 + y) * 4 + x) * 2 + c for y in range(4)] for z in range(8) for x in range(4)] for c in range(2)]
TILE_GROUPS = [[8 * k + t for k in range(4) for t in (q, 7 - q)] for q in range(4)]


def turn_by(angle, quarter):
    square = angle * angle
    sine = 1.0 + square * (-1.0 / 6.0 + square * (1.0 / 120.0 + square * (-1.0 / 5040.0 + square * (1.0 / 362880.0))))
    sine = angle * sine
    cosine = 1.0 + square * (-0.5 + square * (1.0 / 24.0 + square * (-1.0 / 720.0 + square * (1.0 / 40320.0))))
    odd = (quarter & 1) == 1
    first, second = jnp.where(odd, sine, cosine), jnp.where(odd, cosine, sine)
    cosine = jnp.where(((quarter + 1) & 2) == 2, -first, first)
    sine = jnp.where((quarter & 2) == 2, -second, second)
    return cosine, sine


def phases(product):
    turn = product & (N - 1)
    quarter = (turn + N // 8) >> 10
    return turn_by((turn - (quarter << 10)).astype(F32) * (2.0 * math.pi / N), quarter)


def pupil_factor(gap, focus):
    radius = gap * gap * (1.0 / (4.0 * BLOCK * BLOCK))
    amplitude = jnp.exp(-radius)
    angle = focus * radius
    quarter = jnp.floor(angle * (2.0 / math.pi) + 0.5)
    angle = angle - quarter * 1.5703125
    angle = angle - quarter * 4.837512969970703e-4
    angle = angle - quarter * 7.549789954891882e-8
    cosine, sine = turn_by(angle, quarter.astype(jnp.int32))
    return amplitude * cosine, amplitude * sine


def table_kernel(place_ref, rowf_ref, colf_ref):
    first_row, first_column = place_ref[0], place_ref[1]
    u = lax.broadcasted_iota(jnp.int32, (BLOCK, XR), 0) - SPEC // 2
    x = lax.broadcasted_iota(jnp.int32, (BLOCK, XR), 1) + first_row
    y = lax.broadcasted_iota(jnp.int32, (ROWS, BLOCK), 0) + first_column
    lane = lax.broadcasted_iota(jnp.int32, (ROWS, BLOCK), 1)
    v = (lane & 31) * 4 + (lane >> 5) - SPEC // 2

    def body(n, carry):
        cosine, sine = phases((u + n * BLOCK) * x)
        cosine, sine, minus = cosine.astype(BF16), sine.astype(BF16), (-sine).astype(BF16)
        rowf_ref[n, :BLOCK, :XR] = cosine
        rowf_ref[n, :BLOCK, XR:] = sine
        rowf_ref[n, BLOCK:, :XR] = minus
        rowf_ref[n, BLOCK:, XR:] = cosine
        both = jnp.concatenate(phases((v + n * BLOCK) * y), axis=0)
        colf_ref[n, 0] = both.astype(BF16)
        for d in (1, 2, 3):
            colf_ref[n, d] = pltpu.roll(both, 32 * d, 1).astype(BF16)
        return carry

    lax.fori_loop(0, NB, body, 0)
    colf_ref[NB] = jnp.zeros((4, 2 * ROWS, BLOCK), BF16)


def round_bf16(value):
    return value.astype(BF16).astype(F32)


def pack_kernel(core_ref, centers_ref, counts_ref, weights_ref, blocks_ref, spectrum_ref, out_ref):
    start = pl.multiple_of(512 * core_ref[0], 512)
    half = spectrum_ref[:, :, pl.ds(start, 512)].astype(F32).reshape(16, 512).astype(BF16)
    rows = lax.broadcasted_iota(jnp.int32, (BLOCK, BLOCK), 0)
    lanes = lax.broadcasted_iota(jnp.int32, (BLOCK, BLOCK), 1)
    select = (rows == (lanes & 31) * 4 + (lanes >> 5)).astype(F32).astype(BF16)
    parts = [
        jnp.dot(half[:, 128 * j:128 * j + 128], select, preferred_element_type=F32).astype(BF16)
        for j in range(4)
    ]
    numbers = [centers_ref[0, 0], centers_ref[0, 1], counts_ref[0, 0].astype(F32), weights_ref[0, 0]]
    numbers += [blocks_ref[0, k].astype(F32) for k in range(SLOTS)]
    lane = lax.broadcasted_iota(jnp.int32, (16, 128), 1)
    info = jnp.zeros((16, 128), F32)
    for n, value in enumerate(numbers):
        info = jnp.where(lane & 15 == n, value, info)
    high = round_bf16(info)
    mid = round_bf16(info - high)
    low = info - high - mid
    info = jnp.where(lane < 16, high, jnp.where(lane < 32, mid, low)).astype(BF16)
    for n in range(8):
        for j in range(4):
            out_ref[n, j] = parts[j]
        out_ref[n, 4] = info


def spread_kernel(column_ref, out_ref):
    row = lax.broadcasted_iota(jnp.int32, (16, 128), 0)
    info = jnp.zeros((16, 128), F32)
    for n in range(8):
        info = jnp.where(row == n, column_ref[n, 4].astype(F32)[0:1], info)
    info = info.astype(BF16)
    for m in range(4):
        for n in range(8):
            out_ref[m, 4 * n:4 * n + 4] = column_ref[n, :4]
        out_ref[m, 32] = info


def turned_block(rows_ref, at, carrier):
    parts = [
        rows_ref[jnp.where(carrier == 1, 4 * (n % 4) + n // 4, n), at].astype(F32) for n in range(16)
    ]
    stack = jnp.concatenate([p[:8] for p in parts] + [p[8:] for p in parts], axis=0)
    return jnp.transpose(stack.astype(BF16))


def turn_kernel(core_ref, rows_ref, out_ref):
    for n in range(8):
        out_ref[n] = turned_block(rows_ref, n, core_ref[0])


def image_kernel(
    info_ref, whole_ref, focus_ref, core_ref, own_ref, other_ref, rows_ref, columns_ref,
    keep_ref, send_ref, raw, turned, rowf_ref, colf_ref, pieces, power, even, odd, numbers, center_u, center_v, p_re, p_im, q_re, q_im, listing, sems,
):
    def count_of(s):
        return whole_ref[16 * s + 2]

    def block_of(e):
        return whole_ref[((e >> 3) << 4) + 4 + (e & 7)]

    copies = [
        pltpu.make_async_copy(ref, place, sems.at[n])
        for n, (ref, place) in enumerate(
            (
                (other_ref, raw),
                (own_ref, turned.at[pl.ds(0, 32)]),
                (rows_ref, rowf_ref),
                (columns_ref, colf_ref),
            )
        )
    ]
    for copy in copies[:3]:
        copy.start()

    def live(s, total):
        rows = pl.ds(total, SLOTS)
        center_u[rows, :] = jnp.full((SLOTS, BLOCK), info_ref[16 * s])
        center_v[rows, :] = jnp.full((SLOTS, BLOCK), info_ref[16 * s + 1])
        for k in range(SLOTS):
            listing[total + k] = s * SLOTS + k
            numbers[pl.ds(total + k, 1), :] = jnp.full((1, BLOCK), info_ref[16 * s + 4 + k])
        return total + count_of(s)

    total = lax.fori_loop(0, LOCAL, live, 0)
    for n in range(GROUP):
        listing[total + n] = ENTRIES
    groups = (total + GROUP - 1) >> 4
    lane = lax.broadcasted_iota(jnp.int32, (GROUP, BLOCK), 1)
    by_residue = ((lane & 31) * 4 + (lane >> 5)).astype(F32)
    lane = lane.astype(F32)

    def factors(g, carry):
        rows = pl.ds(pl.multiple_of(GROUP * g, GROUP), GROUP)
        number = numbers[rows, :]
        i = jnp.floor(number * (1.0 / NB))
        j = number - i * NB
        p_re[rows, :], p_im[rows, :] = pupil_factor(i * BLOCK + lane - center_u[rows, :], focus_ref[0])
        q_re[rows, :], q_im[rows, :] = pupil_factor(j * BLOCK + by_residue - center_v[rows, :], focus_ref[0])
        return carry

    lax.fori_loop(0, groups, factors, 0)

    pieces[...] = jnp.zeros_like(pieces)
    power[...] = jnp.zeros_like(power)
    copies[0].wait()
    copies[3].start()

    def turn(n, carry):
        for m in range(8):
            turned[32 + 8 * n + m] = turned_block(raw, 8 * n + m, 1 - core_ref[0])
        return carry

    lax.fori_loop(0, 4, turn, 0)
    copies[1].wait()
    copies[2].wait()

    def entries(g, carry):
        places = [listing[g * GROUP + n] for n in range(GROUP)]
        sources = [jnp.minimum(e, ENTRIES - 1) for e in places]
        rows = pl.ds(pl.multiple_of(GROUP * g, GROUP), GROUP)
        pr_all, pi_all = p_re[rows, :], p_im[rows, :]
        q_all = jnp.transpose(jnp.concatenate([q_re[rows, :], q_im[rows, :]], axis=0))
        for n in range(GROUP):
            number = block_of(sources[n])
            i, j = number >> 3, number & 7
            block = turned[(((j >> 2) ^ core_ref[0]) << 5) + (i << 2) + (j & 3)].astype(F32)
            re, im = block[:, :128], block[:, 128:]
            pr, pi = pr_all[n:n + 1], pi_all[n:n + 1]
            qr, qi = q_all[:, n:n + 1], q_all[:, GROUP + n:GROUP + n + 1]
            pupil_re = qr * pr - qi * pi
            pupil_im = qr * pi + qi * pr
            masked_re = (re * pupil_re - im * pupil_im).astype(BF16)
            masked_im = (re * pupil_im + im * pupil_re).astype(BF16)
            masked = jnp.concatenate([masked_re, masked_im], axis=1)
            piece = jnp.dot(masked, rowf_ref[i], preferred_element_type=F32).astype(BF16)
            place = pl.ds(pl.multiple_of(32 * (places[n] & 7), 32), 32)
            for r in range(4):
                pieces[places[n] >> 3, r, place, :] = piece[32 * r:32 * r + 32]
        return carry

    lax.fori_loop(0, groups, entries, 0)
    copies[3].wait()

    lane_group = lax.broadcasted_iota(jnp.int32, (2 * ROWS, 128), 1) // 32

    def transform(s, buffer):
        columns = [
            jnp.where(k < count_of(s), whole_ref[16 * s + 4 + k] & 7, NB) for k in range(SLOTS)
        ]
        for r in range(4):
            halves = []
            for h in range(2):
                table = None
                for m in range(4):
                    term = colf_ref[columns[4 * h + m], (m - r) % 4]
                    table = term if table is None else jnp.where(lane_group == m, term, table)
                halves.append(table)
            table = jnp.concatenate(halves, axis=1)
            buffer[r] = jnp.dot(table, pieces[s, r], preferred_element_type=F32)

    def gather_power(s, buffer):
        weight = info_ref[16 * s + 3]
        for c in range(ROWS // 8):
            low = slice(8 * c, 8 * c + 8)
            high = slice(ROWS + 8 * c, ROWS + 8 * c + 8)
            direct, mirror = [], []
            for r in range(4):
                a_cos, b_cos = buffer[r, low, :128], buffer[r, low, 128:]
                a_sin, b_sin = buffer[r, high, :128], buffer[r, high, 128:]
                direct.append((a_cos - b_sin, a_sin + b_cos))
                mirror.append((a_cos + b_sin, b_cos - a_sin))
            for base, parts in ((0, direct), (4, mirror)):
                (r0, i0), (r1, i1), (r2, i2), (r3, i3) = parts
                gr, gi, dr, di = r0 + r2, i0 + i2, r0 - r2, i0 - i2
                hr, hi, er, ei = r1 + r3, i1 + i3, r1 - r3, i1 - i3
                images = ((gr + hr, gi + hi), (dr - ei, di + er), (gr - hr, gi - hi), (dr + ei, di - er))
                for m, (fr, fi) in enumerate(images):
                    power[base + m, low] += weight * (fr * fr + fi * fi)

    transform(0, even)
    def two(i, carry):
        gather_power(2 * i, even)
        transform(2 * i + 1, odd)
        gather_power(2 * i + 1, odd)
        transform(jnp.minimum(2 * i + 2, LOCAL - 1), even)
        return carry
    lax.fori_loop(0, LOCAL // 2, two, 0)
    mine = pl.multiple_of(PART * core_ref[0], PART)
    theirs = pl.multiple_of(PART * (1 - core_ref[0]), PART)
    for image in range(8):
        keep_ref[image] = power[image, pl.ds(mine, PART_ROWS), :]
        send_ref[image] = power[image, pl.ds(theirs, PART_ROWS), :]


def slope_kernel(dose_ref, keep_ref, other_ref, out_ref):
    dose = dose_ref[0]
    for e in range(8):
        image = e // 2 if e % 2 == 0 else 4 + (e // 2 + 1) % 4
        low = 1 + e % 2
        level = dose * (keep_ref[image] + other_ref[image]) / SOURCES + BACKGROUND
        slope = jnp.abs(level[low + 1:low + 1 + PART] - level[low - 1:low - 1 + PART]) / (
            2.0 * level[low:low + PART]
        )
        out_ref[e] = jnp.exp(slope * (-1.0 / TAU))


def on_device(spectrum, centers, blocks, counts, weights, defocus, dose_scale):
    core = lax.axis_index("cond")
    source = lax.axis_index("source")
    z, y = source // 4, source % 4
    swap = [(0, 1), (1, 0)]
    vmem = pl.BlockSpec(memory_space=pltpu.VMEM)
    smem = pl.BlockSpec(memory_space=pltpu.SMEM)
    hbm = pl.BlockSpec(memory_space=pl.ANY)
    packed = pl.pallas_call(
        pack_kernel,
        out_shape=jax.ShapeDtypeStruct((8, 5, 16, 128), BF16),
        in_specs=[smem] * 5 + [vmem],
        out_specs=vmem,
        compiler_params=pltpu.CompilerParams(vmem_limit_bytes=56 * MIB),
    )(core.reshape(1), centers, counts.reshape(1, 1), weights.reshape(1, 1), blocks, spectrum)
    column = lax.all_to_all(packed, "source", 0, 0, axis_index_groups=Z_GROUPS)
    defocus, dose_scale, column = lax.optimization_barrier((defocus, dose_scale, column))

    local = jnp.concatenate([defocus, dose_scale])
    remote = lax.ppermute(local, "cond", swap)
    cond = z % 4
    chosen = jnp.where(cond // 2 == core, local, remote)
    focus = jnp.where(cond % 2 == 0, chosen[0], chosen[1])
    dose = jnp.where(cond % 2 == 0, chosen[2], chosen[3])
    quarter = jnp.where(z % 2 == 0, y, 3 - y)
    window = 2 * quarter + z // 4
    place = jnp.stack([lax.axis_index("row") * XR, window * W - 1])
    place, column = lax.optimization_barrier((place, column))
    rowf, colf = pl.pallas_call(
        table_kernel,
        out_shape=[
            jax.ShapeDtypeStruct((NB, 2 * BLOCK, 2 * XR), BF16),
            jax.ShapeDtypeStruct((NB + 1, 4, 2 * ROWS, BLOCK), BF16),
        ],
        in_specs=[smem],
        out_specs=[vmem, vmem],
        compiler_params=pltpu.CompilerParams(vmem_limit_bytes=56 * MIB),
    )(place)

    copies = pl.pallas_call(
        spread_kernel,
        out_shape=jax.ShapeDtypeStruct((4, 33, 16, 128), BF16),
        in_specs=[vmem],
        out_specs=vmem,
        compiler_params=pltpu.CompilerParams(vmem_limit_bytes=4 * MIB),
    )(column)
    every = ("source", "row", "cond")
    line = lax.all_to_all(copies, every, 0, 0, axis_index_groups=X_LINES[0] + Y_LINES[1])
    line, rowf, colf, dose, focus = lax.optimization_barrier((line, rowf, colf, dose, focus))
    copies = jnp.broadcast_to(line[None], (4, 4, 33, 16, 128))
    rows = lax.all_to_all(copies, every, 0, 0, axis_index_groups=Y_LINES[0] + X_LINES[1])
    rows = rows.reshape(16, 33, 16, 128)
    own = pl.pallas_call(
        turn_kernel,
        grid=(4,),
        out_shape=jax.ShapeDtypeStruct((32, 128, 256), BF16),
        in_specs=[smem, pl.BlockSpec((16, 8, 16, 128), lambda i: (0, i, 0, 0))],
        out_specs=pl.BlockSpec((8, 128, 256), lambda i: (i, 0, 0)),
        compiler_params=pltpu.CompilerParams(vmem_limit_bytes=8 * MIB),
    )(core.reshape(1), rows)
    other = lax.ppermute(rows, "cond", swap)

    tiles = rows[:5, 32, :8, :48]
    info = jnp.stack([jnp.where(core == 0, tiles[0], tiles[2]), jnp.where(core == 0, tiles[4], tiles[3])]).astype(F32)
    info = (info[:, :, :16] + info[:, :, 16:32] + info[:, :, 32:]).reshape(-1)
    keep, send = pl.pallas_call(
        image_kernel,
        out_shape=[jax.ShapeDtypeStruct((8, PART_ROWS, XR), F32)] * 2,
        in_specs=[smem] * 4 + [hbm] * 4,
        out_specs=[vmem] * 2,
        scratch_shapes=[
            pltpu.VMEM((16, 33, 16, 128), BF16),
            pltpu.VMEM((64, 128, 256), BF16),
            pltpu.VMEM((NB, 2 * BLOCK, 2 * XR), BF16),
            pltpu.VMEM((NB + 1, 4, 2 * ROWS, BLOCK), BF16),
            pltpu.VMEM((LOCAL + 1, 4, 256, 256), BF16),
            pltpu.VMEM((8, ROWS, XR), F32),
            pltpu.VMEM((4, 2 * ROWS, 256), F32),
            pltpu.VMEM((4, 2 * ROWS, 256), F32),
        ] + [pltpu.VMEM((ENTRIES + SLOTS, BLOCK), F32)] * 7 + [
            pltpu.SMEM((ENTRIES + GROUP,), jnp.int32),
            pltpu.SemaphoreType.DMA((4,)),
        ],
        compiler_params=pltpu.CompilerParams(vmem_limit_bytes=52 * MIB),
    )(info, info.astype(jnp.int32), focus.reshape(1), core.reshape(1), own, other, rowf, colf)
    received = lax.ppermute(send, "cond", swap)
    terms = pl.pallas_call(
        slope_kernel,
        out_shape=jax.ShapeDtypeStruct((8, PART, XR), F32),
        in_specs=[smem, vmem, vmem],
        out_specs=vmem,
        compiler_params=pltpu.CompilerParams(vmem_limit_bytes=4 * MIB),
    )(dose.reshape(1), keep, received)
    terms = lax.all_to_all(terms, "source", 0, 0, axis_index_groups=TILE_GROUPS)
    soft = -TAU * jnp.log(jnp.sum(terms.reshape(2, CONDS, PART, XR), axis=1) / CONDS)
    theirs = lax.ppermute(soft, "cond", swap)
    first, second = jnp.where(core == 0, soft, theirs), jnp.where(core == 0, theirs, soft)
    soft = jnp.stack([first, second], axis=1).reshape(2 * W, XR)
    soft = jnp.where(z % 2 == 0, soft, soft[::-1])
    return soft.T


def solution(mesh):
    in_specs = (
        P(None, ("source", "row"), None),
        P("source", None),
        P("source", None),
        P("source"),
        P("source"),
        P("cond"),
        P("cond"),
    )
    out_specs = P("row", "source")
    return jax.shard_map(
        on_device, mesh=mesh, in_specs=in_specs, out_specs=out_specs, check_vma=False
    )
```

```python
import functools
import math

import jax
import jax.numpy as jnp
from jax import lax
from jax.experimental import pallas as pl
from jax.experimental.pallas import tpu as pltpu
from jax.sharding import PartitionSpec as P

N = 4096
BLOCK = 128
NB = 8
XR = 128
SPEC = 1024
SOURCES = 32
SLOTS = 8
CONDS = 4
W = 64
ROWS = 72
PART = 32
PART_ROWS = 40
GROUP = 16
LOCAL = SOURCES // 2
ENTRIES = LOCAL * SLOTS

TAU = 0.5
BACKGROUND = 0.05

MIB = 1024 * 1024
F32 = jnp.float32
BF16 = jnp.bfloat16

Z_GROUPS = [[z * 4 + y for z in range(8)] for y in range(4)]
X_LINES = [[[((z * 4 + y) * 4 + x) * 2 + c for x in range(4)] for z in range(8) for y in range(4)] for c in range(2)]
Y_LINES = [[[((z * 4 + y) * 4 + x) * 2 + c for y in range(4)] for z in range(8) for x in range(4)] for c in range(2)]
TILE_GROUPS = [[8 * k + t for k in range(4) for t in (q, 7 - q)] for q in range(4)]


def turn_by(angle, quarter):
    square = angle * angle
    sine = 1.0 + square * (-1.0 / 6.0 + square * (1.0 / 120.0 + square * (-1.0 / 5040.0 + square * (1.0 / 362880.0))))
    sine = angle * sine
    cosine = 1.0 + square * (-0.5 + square * (1.0 / 24.0 + square * (-1.0 / 720.0 + square * (1.0 / 40320.0))))
    odd = (quarter & 1) == 1
    first, second = jnp.where(odd, sine, cosine), jnp.where(odd, cosine, sine)
    cosine = jnp.where(((quarter + 1) & 2) == 2, -first, first)
    sine = jnp.where((quarter & 2) == 2, -second, second)
    return cosine, sine


def phases(product):
    turn = product & (N - 1)
    quarter = (turn + N // 8) >> 10
    return turn_by((turn - (quarter << 10)).astype(F32) * (2.0 * math.pi / N), quarter)


def pupil_factor(gap, focus):
    radius = gap * gap * (1.0 / (4.0 * BLOCK * BLOCK))
    amplitude = jnp.exp(-radius)
    angle = focus * radius
    quarter = jnp.floor(angle * (2.0 / math.pi) + 0.5)
    angle = angle - quarter * 1.5703125
    angle = angle - quarter * 4.837512969970703e-4
    angle = angle - quarter * 7.549789954891882e-8
    cosine, sine = turn_by(angle, quarter.astype(jnp.int32))
    return amplitude * cosine, amplitude * sine


def table_kernel(place_ref, rowf_ref, colf_ref):
    first_row, first_column = place_ref[0], place_ref[1]
    u = lax.broadcasted_iota(jnp.int32, (BLOCK, XR), 0) - SPEC // 2
    x = lax.broadcasted_iota(jnp.int32, (BLOCK, XR), 1) + first_row
    y = lax.broadcasted_iota(jnp.int32, (ROWS, BLOCK), 0) + first_column
    lane = lax.broadcasted_iota(jnp.int32, (ROWS, BLOCK), 1)
    v = (lane & 31) * 4 + (lane >> 5) - SPEC // 2

    def body(n, carry):
        cosine, sine = phases((u + n * BLOCK) * x)
        cosine, sine, minus = cosine.astype(BF16), sine.astype(BF16), (-sine).astype(BF16)
        rowf_ref[n, :BLOCK, :XR] = cosine
        rowf_ref[n, :BLOCK, XR:] = sine
        rowf_ref[n, BLOCK:, :XR] = minus
        rowf_ref[n, BLOCK:, XR:] = cosine
        both = jnp.concatenate(phases((v + n * BLOCK) * y), axis=0)
        colf_ref[n, 0] = both.astype(BF16)
        for d in (1, 2, 3):
            colf_ref[n, d] = pltpu.roll(both, 32 * d, 1).astype(BF16)
        return carry

    lax.fori_loop(0, NB, body, 0)
    colf_ref[NB] = jnp.zeros((4, 2 * ROWS, BLOCK), BF16)


def round_bf16(value):
    return value.astype(BF16).astype(F32)


def pack_kernel(core_ref, centers_ref, counts_ref, weights_ref, blocks_ref, spectrum_ref, out_ref):
    start = pl.multiple_of(512 * core_ref[0], 512)
    half = spectrum_ref[:, :, pl.ds(start, 512)].astype(F32).reshape(16, 512).astype(BF16)
    rows = lax.broadcasted_iota(jnp.int32, (BLOCK, BLOCK), 0)
    lanes = lax.broadcasted_iota(jnp.int32, (BLOCK, BLOCK), 1)
    select = (rows == (lanes & 31) * 4 + (lanes >> 5)).astype(F32).astype(BF16)
    parts = [
        jnp.dot(half[:, 128 * j:128 * j + 128], select, preferred_element_type=F32).astype(BF16)
        for j in range(4)
    ]
    numbers = [centers_ref[0, 0], centers_ref[0, 1], counts_ref[0, 0].astype(F32), weights_ref[0, 0]]
    numbers += [blocks_ref[0, k].astype(F32) for k in range(SLOTS)]
    lane = lax.broadcasted_iota(jnp.int32, (16, 128), 1)
    info = jnp.zeros((16, 128), F32)
    for n, value in enumerate(numbers):
        info = jnp.where(lane & 15 == n, value, info)
    high = round_bf16(info)
    mid = round_bf16(info - high)
    low = info - high - mid
    info = jnp.where(lane < 16, high, jnp.where(lane < 32, mid, low)).astype(BF16)
    for n in range(8):
        for j in range(4):
            out_ref[n, j] = parts[j]
        out_ref[n, 4] = info


def spread_kernel(column_ref, out_ref):
    row = lax.broadcasted_iota(jnp.int32, (16, 128), 0)
    info = jnp.zeros((16, 128), F32)
    for n in range(8):
        info = jnp.where(row == n, column_ref[n, 4].astype(F32)[0:1], info)
    info = info.astype(BF16)
    for m in range(4):
        for n in range(8):
            out_ref[m, 4 * n:4 * n + 4] = column_ref[n, :4]
        out_ref[m, 32] = info


def turned_block(rows_ref, at, carrier):
    parts = [
        rows_ref[jnp.where(carrier == 1, 4 * (n % 4) + n // 4, n), at].astype(F32) for n in range(16)
    ]
    stack = jnp.concatenate([p[:8] for p in parts] + [p[8:] for p in parts], axis=0)
    return jnp.transpose(stack.astype(BF16))


def turn_kernel(core_ref, rows_ref, out_ref):
    for n in range(8):
        out_ref[n] = turned_block(rows_ref, n, core_ref[0])


def image_kernel(
    info_ref, whole_ref, focus_ref, core_ref, own_ref, other_ref, rows_ref, columns_ref,
    keep_ref, send_ref, raw, turned, rowf_ref, colf_ref, pieces, power, even, odd, numbers, center_u, center_v, p_re, p_im, q_re, q_im, listing, sems,
):
    def count_of(s):
        return whole_ref[16 * s + 2]

    def block_of(e):
        return whole_ref[((e >> 3) << 4) + 4 + (e & 7)]

    copies = [
        pltpu.make_async_copy(ref, place, sems.at[n])
        for n, (ref, place) in enumerate(
            (
                (other_ref, raw),
                (own_ref, turned.at[pl.ds(0, 32)]),
                (rows_ref, rowf_ref),
                (columns_ref, colf_ref),
            )
        )
    ]
    for copy in copies[:3]:
        copy.start()

    def live(s, total):
        rows = pl.ds(total, SLOTS)
        center_u[rows, :] = jnp.full((SLOTS, BLOCK), info_ref[16 * s])
        center_v[rows, :] = jnp.full((SLOTS, BLOCK), info_ref[16 * s + 1])
        for k in range(SLOTS):
            listing[total + k] = s * SLOTS + k
            numbers[pl.ds(total + k, 1), :] = jnp.full((1, BLOCK), info_ref[16 * s + 4 + k])
        return total + count_of(s)

    total = lax.fori_loop(0, LOCAL, live, 0)
    for n in range(GROUP):
        listing[total + n] = ENTRIES
    groups = (total + GROUP - 1) >> 4
    lane = lax.broadcasted_iota(jnp.int32, (GROUP, BLOCK), 1)
    by_residue = ((lane & 31) * 4 + (lane >> 5)).astype(F32)
    lane = lane.astype(F32)

    def factors(g, carry):
        rows = pl.ds(pl.multiple_of(GROUP * g, GROUP), GROUP)
        number = numbers[rows, :]
        i = jnp.floor(number * (1.0 / NB))
        j = number - i * NB
        p_re[rows, :], p_im[rows, :] = pupil_factor(i * BLOCK + lane - center_u[rows, :], focus_ref[0])
        q_re[rows, :], q_im[rows, :] = pupil_factor(j * BLOCK + by_residue - center_v[rows, :], focus_ref[0])
        return carry

    lax.fori_loop(0, groups, factors, 0)

    pieces[...] = jnp.zeros_like(pieces)
    power[...] = jnp.zeros_like(power)
    copies[0].wait()
    copies[3].start()

    def turn(n, carry):
        for m in range(8):
            turned[32 + 8 * n + m] = turned_block(raw, 8 * n + m, 1 - core_ref[0])
        return carry

    lax.fori_loop(0, 4, turn, 0)
    copies[1].wait()
    copies[2].wait()

    def entries(g, carry):
        places = [listing[g * GROUP + n] for n in range(GROUP)]
        sources = [jnp.minimum(e, ENTRIES - 1) for e in places]
        rows = pl.ds(pl.multiple_of(GROUP * g, GROUP), GROUP)
        pr_all, pi_all = p_re[rows, :], p_im[rows, :]
        q_all = jnp.transpose(jnp.concatenate([q_re[rows, :], q_im[rows, :]], axis=0))
        for n in range(GROUP):
            number = block_of(sources[n])
            i, j = number >> 3, number & 7
            block = turned[(((j >> 2) ^ core_ref[0]) << 5) + (i << 2) + (j & 3)].astype(F32)
            re, im = block[:, :128], block[:, 128:]
            pr, pi = pr_all[n:n + 1], pi_all[n:n + 1]
            qr, qi = q_all[:, n:n + 1], q_all[:, GROUP + n:GROUP + n + 1]
            pupil_re = qr * pr - qi * pi
            pupil_im = qr * pi + qi * pr
            masked_re = (re * pupil_re - im * pupil_im).astype(BF16)
            masked_im = (re * pupil_im + im * pupil_re).astype(BF16)
            masked = jnp.concatenate([masked_re, masked_im], axis=1)
            piece = jnp.dot(masked, rowf_ref[i], preferred_element_type=F32).astype(BF16)
            place = pl.ds(pl.multiple_of(32 * (places[n] & 7), 32), 32)
            for r in range(4):
                pieces[places[n] >> 3, r, place, :] = piece[32 * r:32 * r + 32]
        return carry

    lax.fori_loop(0, groups, entries, 0)
    copies[3].wait()

    lane_group = lax.broadcasted_iota(jnp.int32, (2 * ROWS, 128), 1) // 32

    def transform(s, buffer):
        columns = [
            jnp.where(k < count_of(s), whole_ref[16 * s + 4 + k] & 7, NB) for k in range(SLOTS)
        ]
        for r in range(4):
            halves = []
            for h in range(2):
                table = None
                for m in range(4):
                    term = colf_ref[columns[4 * h + m], (m - r) % 4]
                    table = term if table is None else jnp.where(lane_group == m, term, table)
                halves.append(table)
            table = jnp.concatenate(halves, axis=1)
            buffer[r] = jnp.dot(table, pieces[s, r], preferred_element_type=F32)

    def gather_power(s, buffer):
        weight = info_ref[16 * s + 3]
        for c in range(ROWS // 8):
            low = slice(8 * c, 8 * c + 8)
            high = slice(ROWS + 8 * c, ROWS + 8 * c + 8)
            direct, mirror = [], []
            for r in range(4):
                a_cos, b_cos = buffer[r, low, :128], buffer[r, low, 128:]
                a_sin, b_sin = buffer[r, high, :128], buffer[r, high, 128:]
                direct.append((a_cos - b_sin, a_sin + b_cos))
                mirror.append((a_cos + b_sin, b_cos - a_sin))
            for base, parts in ((0, direct), (4, mirror)):
                (r0, i0), (r1, i1), (r2, i2), (r3, i3) = parts
                gr, gi, dr, di = r0 + r2, i0 + i2, r0 - r2, i0 - i2
                hr, hi, er, ei = r1 + r3, i1 + i3, r1 - r3, i1 - i3
                images = ((gr + hr, gi + hi), (dr - ei, di + er), (gr - hr, gi - hi), (dr + ei, di - er))
                for m, (fr, fi) in enumerate(images):
                    power[base + m, low] += weight * (fr * fr + fi * fi)

    transform(0, even)
    def two(i, carry):
        gather_power(2 * i, even)
        transform(2 * i + 1, odd)
        gather_power(2 * i + 1, odd)
        transform(jnp.minimum(2 * i + 2, LOCAL - 1), even)
        return carry
    lax.fori_loop(0, LOCAL // 2, two, 0)
    mine = pl.multiple_of(PART * core_ref[0], PART)
    theirs = pl.multiple_of(PART * (1 - core_ref[0]), PART)
    for image in range(8):
        keep_ref[image] = power[image, pl.ds(mine, PART_ROWS), :]
        send_ref[image] = power[image, pl.ds(theirs, PART_ROWS), :]


def slope_kernel(dose_ref, keep_ref, other_ref, out_ref):
    dose = dose_ref[0]
    for e in range(8):
        image = e // 2 if e % 2 == 0 else 4 + (e // 2 + 1) % 4
        low = 1 + e % 2
        level = dose * (keep_ref[image] + other_ref[image]) / SOURCES + BACKGROUND
        slope = jnp.abs(level[low + 1:low + 1 + PART] - level[low - 1:low - 1 + PART]) / (
            2.0 * level[low:low + PART]
        )
        out_ref[e] = jnp.exp(slope * (-1.0 / TAU))


def on_device(spectrum, centers, blocks, counts, weights, defocus, dose_scale):
    core = lax.axis_index("cond")
    source = lax.axis_index("source")
    z, y = source // 4, source % 4
    swap = [(0, 1), (1, 0)]
    vmem = pl.BlockSpec(memory_space=pltpu.VMEM)
    smem = pl.BlockSpec(memory_space=pltpu.SMEM)
    hbm = pl.BlockSpec(memory_space=pl.ANY)
    packed = pl.pallas_call(
        pack_kernel,
        out_shape=jax.ShapeDtypeStruct((8, 5, 16, 128), BF16),
        in_specs=[smem] * 5 + [vmem],
        out_specs=vmem,
        compiler_params=pltpu.CompilerParams(vmem_limit_bytes=56 * MIB),
    )(core.reshape(1), centers, counts.reshape(1, 1), weights.reshape(1, 1), blocks, spectrum)
    column = lax.all_to_all(packed, "source", 0, 0, axis_index_groups=Z_GROUPS)
    defocus, dose_scale, column = lax.optimization_barrier((defocus, dose_scale, column))

    local = jnp.concatenate([defocus, dose_scale])
    remote = lax.ppermute(local, "cond", swap)
    cond = z % 4
    chosen = jnp.where(cond // 2 == core, local, remote)
    focus = jnp.where(cond % 2 == 0, chosen[0], chosen[1])
    dose = jnp.where(cond % 2 == 0, chosen[2], chosen[3])
    quarter = jnp.where(z % 2 == 0, y, 3 - y)
    window = 2 * quarter + z // 4
    place = jnp.stack([lax.axis_index("row") * XR, window * W - 1])
    place, column = lax.optimization_barrier((place, column))
    rowf, colf = pl.pallas_call(
        table_kernel,
        out_shape=[
            jax.ShapeDtypeStruct((NB, 2 * BLOCK, 2 * XR), BF16),
            jax.ShapeDtypeStruct((NB + 1, 4, 2 * ROWS, BLOCK), BF16),
        ],
        in_specs=[smem],
        out_specs=[vmem, vmem],
        compiler_params=pltpu.CompilerParams(vmem_limit_bytes=8 * MIB),
    )(place)

    copies = pl.pallas_call(
        spread_kernel,
        out_shape=jax.ShapeDtypeStruct((4, 33, 16, 128), BF16),
        in_specs=[vmem],
        out_specs=vmem,
        compiler_params=pltpu.CompilerParams(vmem_limit_bytes=4 * MIB),
    )(column)
    every = ("source", "row", "cond")
    line = lax.all_to_all(copies, every, 0, 0, axis_index_groups=X_LINES[0] + Y_LINES[1])
    line, rowf, colf, dose, focus = lax.optimization_barrier((line, rowf, colf, dose, focus))
    copies = jnp.broadcast_to(line[None], (4, 4, 33, 16, 128))
    rows = lax.all_to_all(copies, every, 0, 0, axis_index_groups=Y_LINES[0] + X_LINES[1])
    rows = rows.reshape(16, 33, 16, 128)
    own = pl.pallas_call(
        turn_kernel,
        grid=(4,),
        out_shape=jax.ShapeDtypeStruct((32, 128, 256), BF16),
        in_specs=[smem, pl.BlockSpec((16, 8, 16, 128), lambda i: (0, i, 0, 0))],
        out_specs=pl.BlockSpec((8, 128, 256), lambda i: (i, 0, 0)),
        compiler_params=pltpu.CompilerParams(vmem_limit_bytes=8 * MIB),
    )(core.reshape(1), rows)
    other = lax.ppermute(rows, "cond", swap)

    tiles = rows[:5, 32, :8, :48]
    info = jnp.stack([jnp.where(core == 0, tiles[0], tiles[2]), jnp.where(core == 0, tiles[4], tiles[3])]).astype(F32)
    info = (info[:, :, :16] + info[:, :, 16:32] + info[:, :, 32:]).reshape(-1)
    keep, send = pl.pallas_call(
        image_kernel,
        out_shape=[jax.ShapeDtypeStruct((8, PART_ROWS, XR), F32)] * 2,
        in_specs=[smem] * 4 + [hbm] * 4,
        out_specs=[vmem] * 2,
        scratch_shapes=[
            pltpu.VMEM((16, 33, 16, 128), BF16),
            pltpu.VMEM((64, 128, 256), BF16),
            pltpu.VMEM((NB, 2 * BLOCK, 2 * XR), BF16),
            pltpu.VMEM((NB + 1, 4, 2 * ROWS, BLOCK), BF16),
            pltpu.VMEM((LOCAL + 1, 4, 256, 256), BF16),
            pltpu.VMEM((8, ROWS, XR), F32),
            pltpu.VMEM((4, 2 * ROWS, 256), F32),
            pltpu.VMEM((4, 2 * ROWS, 256), F32),
        ] + [pltpu.VMEM((ENTRIES + SLOTS, BLOCK), F32)] * 7 + [
            pltpu.SMEM((ENTRIES + GROUP,), jnp.int32),
            pltpu.SemaphoreType.DMA((4,)),
        ],
        compiler_params=pltpu.CompilerParams(vmem_limit_bytes=52 * MIB),
    )(info, info.astype(jnp.int32), focus.reshape(1), core.reshape(1), own, other, rowf, colf)
    received = lax.ppermute(send, "cond", swap)
    terms = pl.pallas_call(
        slope_kernel,
        out_shape=jax.ShapeDtypeStruct((8, PART, XR), F32),
        in_specs=[smem, vmem, vmem],
        out_specs=vmem,
        compiler_params=pltpu.CompilerParams(vmem_limit_bytes=4 * MIB),
    )(dose.reshape(1), keep, received)
    terms = lax.all_to_all(terms, "source", 0, 0, axis_index_groups=TILE_GROUPS)
    soft = -TAU * jnp.log(jnp.sum(terms.reshape(2, CONDS, PART, XR), axis=1) / CONDS)
    theirs = lax.ppermute(soft, "cond", swap)
    first, second = jnp.where(core == 0, soft, theirs), jnp.where(core == 0, theirs, soft)
    soft = jnp.stack([first, second], axis=1).reshape(2 * W, XR)
    soft = jnp.where(z % 2 == 0, soft, soft[::-1])
    return soft.T


def solution(mesh):
    in_specs = (
        P(None, ("source", "row"), None),
        P("source", None),
        P("source", None),
        P("source"),
        P("source"),
        P("cond"),
        P("cond"),
    )
    out_specs = P("row", "source")
    return jax.shard_map(
        on_device, mesh=mesh, in_specs=in_specs, out_specs=out_specs, check_vma=False
    )
```
